32 devices in a mesh: grp: 2 (over y), band: 4 (over z), tm: 2 (over x), chan: 2 (over core).
Axes of the slice: x: 2, y: 2, z: 4, core: 2. Of those that a mesh axis runs over, the one named last changes fastest.
Arguments:
- tdi_data: float32 [4, 512, 128, 128], P(('grp', 'chan'), 'band', 'tm'), parts along dimension 0, may hold values from -6 to 6
- noise_diag: float32 [4, 512, 128, 128], P(('grp', 'chan'), 'band', 'tm'), parts along dimension 0, may hold values from 0.17 to 11.3
- noise_off: float32 [4, 512, 128, 128], P(('grp', 'chan'), 'band', 'tm'), parts along dimension 0, may hold values from -2.6 to 2.6
- src_blocks: bfloat16 [16384, 2, 128], P(('grp', 'band', 'tm'), 'chan'), parts along dimension 0, may hold values from -3 to 3
- owner_dev: int32 [16384, 1], P(('grp', 'band', 'tm')), parts along dimension 0, may hold values from 0 to 7; in each aligned block of 1024 rows (0 to 1023, 1024 to 2047, ...) at most 256 rows name the same one
- layer_in: int32 [16384], P(('grp', 'band', 'tm')), parts along dimension 0, may hold values from 0 to 127
- seg_in: int32 [16384], P(('grp', 'band', 'tm')), parts along dimension 0, may hold values from 0 to 63
Outputs:
- weighted: float32 [4, 512, 128, 128], P(('grp', 'chan'), 'band', 'tm'), parts along dimension 0
- log_like: float32 [2], P('grp'), parts along dimension 0
- grad_blocks: bfloat16 [16384, 2, 128], P(('grp', 'band', 'tm'), 'chan'), parts along dimension 0
The draws below stay inside these ranges and needn't reach their ends.
There are 2 independent parts, one for each index of `grp`. The reference program is written for one: setup_inputs(seed, part) draws one part's arguments, and reference() takes and returns one part's arrays. A program takes and returns all parts, laid end to end along the dimension named above; each array names one. Nothing has to cross between parts.
Inputs may be any that keep to these rules, and one draw needn't show every extreme that they name: `owner_dev`: of the 1024 rows of one device (aligned blocks of 1024 rows), at most 256 name the same owner, and in every draw some owner is named by exactly 256 rows of one device.
All inputs are finite; a program needn't handle non-finite values.
Results may differ from the reference program's by a relative error of at most 0.0004.
Values may be sent and summed in bfloat16 or wider, within the bound.
No kernel may reach another device: no remote copies, remote signals or barrier semaphores. Data moves between devices by JAX's collectives and lax.ppermute only.
A program may use at most 64 MiB of HBM per device.

```python
import math
import jax
import jax.numpy as jnp
import numpy as np

C = 2
NF = 512
NT = 16384
K = 128
SRC_DEV = 1024
NSEG = 128
LB = 128
SEG_TM = 64
SOURCES = 8192
CAP = 256
N_BAND = 4
N_TM = 2


def noise_scale(time_tilt):
    row_frac = jnp.arange(NF, dtype=jnp.float32).reshape(1, NF, 1, 1) / NF
    col_frac = jnp.arange(NSEG, dtype=jnp.float32).reshape(1, 1, NSEG, 1) / NSEG
    return 10.0 ** (row_frac - 0.5 + time_tilt * (col_frac - 0.5))


def draw_noise_diag(key, part):
    key = jax.random.fold_in(key, 11)
    full_shape = (C, NF, NSEG, K)
    factor = 1.0 + jax.random.uniform(key, full_shape, jnp.float32)
    return noise_scale(0.0) * factor


def draw_noise_off(key, part):
    key = jax.random.fold_in(key, 23)
    full_shape = (C, NF, NSEG, K)
    factor = jnp.clip(0.2 * jax.random.normal(key, full_shape, jnp.float32), -0.45, 0.45)
    return noise_scale(0.0) * factor


def place_ends(result, stream_key, least, top_value):
    longest = result.shape.index(max(result.shape))
    spots = []
    for shift in (0, 1):
        where = [jax.random.randint(jax.random.fold_in(stream_key, axis), (), 0, length) for axis, length in enumerate(result.shape)]
        where[longest] = (where[longest] + shift) % result.shape[longest]
        spots.append(tuple(where))
    return result.at[spots[0]].set(least).at[spots[1]].set(top_value)


def block_levels(own_key, dims, shards, low, high):
    factor_of, own = 1.0, jax.random.fold_in(own_key, 6)
    for axis_at, parts in shards:
        steps = jnp.exp(jax.random.uniform(jax.random.fold_in(own, axis_at), (parts,), jnp.float32, low / len(shards), high / len(shards)))
        factor_of = factor_of * jnp.repeat(steps, dims[axis_at] // parts).reshape([-1 if axis == axis_at else 1 for axis in range(len(dims))])
    return factor_of


def assign_block(rng, own, number, rows, count, top, bound, slope):
    sequence = jax.random.permutation(rng, count)
    packed, usual = portions_of(count, rows * top, bound, slope, True), portions_of(count, rows * top, bound, slope, False)
    places = jnp.arange(count)

    def named(tallies, turn):
        used = int((tallies > 0).sum())
        fixed = max(1, used // 4)
        shifted = fixed + (places - fixed + turn * (used - fixed)) % max(1, count - fixed)
        return jnp.zeros((count,), jnp.int32).at[sequence[jnp.where(places < fixed, places, shifted)]].set(jnp.asarray(tallies, jnp.int32))

    tallies = jnp.where(number % 4 == 0, named(packed, number // 4), named(usual, number - number // 4 - 1))
    mixed = jax.random.permutation(jax.random.fold_in(own, 3), count)
    source_of, receiver = mixed[0:count // 2 * 2:2], mixed[1:count // 2 * 2:2]
    slack = jnp.minimum(tallies[source_of] - 1, bound - tallies[receiver]) // 2
    slack = jnp.where((source_of == sequence[0]) | (receiver == sequence[0]) | (tallies[receiver] == 0), 0, jnp.maximum(slack, 0))
    shifted = jax.random.randint(jax.random.fold_in(own, 4), (count // 2,), 0, 1 << 20) % (slack + 1)
    tallies = tallies.at[source_of].add(-shifted).at[receiver].add(shifted)
    items = jnp.searchsorted(jnp.cumsum(tallies), jnp.arange(rows * top), side="right").astype(jnp.int32)
    table = items.reshape(top, rows).T
    table = table[jax.random.permutation(jax.random.fold_in(own, 1), rows)]
    turn = jax.random.randint(jax.random.fold_in(own, 2), (rows, 1), 0, top)
    return jnp.take_along_axis(table, (jnp.arange(top)[None, :] + turn) % top, axis=1)


def portions_of(amount, total, reach, skew, full):
    portions = [(1 << 20) // math.isqrt(grade ** skew) + 1 for grade in range(1, amount + 1)]
    largest = reach if full else min(reach, max(-(-total // amount), total * portions[0] // sum(portions)))
    least = 1 if total - largest >= amount - 1 else 0
    counts, rest = [largest] + [least] * (amount - 1), total - largest - least * (amount - 1)
    while rest > 0:
        movable = [i for i in range(1, amount) if counts[i] < largest] or [i for i in range(1, amount) if counts[i] < reach]
        whole, left = sum([portions[i] for i in movable]), rest
        for i in movable:
            addition = min(reach - counts[i], max(1, left * portions[i] // whole), rest)
            counts[i] = counts[i] + addition
            rest = rest - addition
    return np.array(counts)


def bell_draw(stream_key, dims, deviation, limit, cuts=(), kind=jnp.bfloat16):
    array = jax.random.normal(stream_key, dims, jnp.float32) * deviation
    if len(cuts) > 0:
        array = block_levels(stream_key, dims, cuts, -0.22, 0.18) * array
    return jnp.clip(array, min=-limit, max=limit).astype(kind)


def setup_inputs(seed: int = 0, part: int = 0) -> dict:
    splits = jax.random.split(jax.random.key(seed), 8)
    part_keys = jax.random.split(jax.random.fold_in(splits[7], part), 8)
    tdi_data = bell_draw(part_keys[0], (C, NF, NSEG, K), 1.0, 6.0, ((0, 2), (1, 4), (2, 2)), jnp.float32)
    noise_diag = draw_noise_diag(jax.random.fold_in(jax.random.fold_in(splits[7], part), 71), part)
    noise_off = draw_noise_off(jax.random.fold_in(jax.random.fold_in(splits[7], part), 71), part)
    src_blocks = bell_draw(part_keys[3], (SOURCES, C, K), 0.5, 3.0, ((0, 8), (1, 2)))
    owner_dev_keys = jax.random.split(jax.random.fold_in(part_keys[4], 1), SOURCES // SRC_DEV)
    owner_dev_turns = jax.random.permutation(jax.random.fold_in(part_keys[4], 3), SOURCES // SRC_DEV)
    owner_dev = jax.vmap(lambda own, number: assign_block(jax.random.fold_in(part_keys[4], 2), own, number, SRC_DEV, N_BAND * N_TM, 1, CAP, 2))(owner_dev_keys, owner_dev_turns).reshape((SOURCES, 1))
    layer_in = place_ends(jax.random.randint(part_keys[5], (SOURCES,), 0, LB), jax.random.fold_in(part_keys[5], 1), 0, LB - 1).astype(jnp.int32)
    seg_in = place_ends(jax.random.randint(part_keys[6], (SOURCES,), 0, SEG_TM), jax.random.fold_in(part_keys[6], 1), 0, SEG_TM - 1).astype(jnp.int32)
    return dict(tdi_data=tdi_data, noise_diag=noise_diag, noise_off=noise_off, src_blocks=src_blocks, owner_dev=owner_dev, layer_in=layer_in, seg_in=seg_in)


def apply_noise(residual, diag_part, off_part):
    product = off_part * residual
    upper_rim = jnp.pad(residual[:, 1:], ((0, 0), (0, 1), (0, 0), (0, 0)))
    lower_rim = jnp.pad(product[:, :-1], ((0, 0), (1, 0), (0, 0), (0, 0)))
    return diag_part * residual + off_part * upper_rim + lower_rim


def reference(tdi_data, noise_diag, noise_off, src_blocks, owner_dev, layer_in, seg_in):
    owner_id = owner_dev[:, 0]
    layer_idx = (owner_id // N_TM) * LB + layer_in
    segment = (owner_id % N_TM) * SEG_TM + seg_in
    cell_ids = (layer_idx * NSEG + segment).astype(jnp.int32)
    blocks = src_blocks.astype(jnp.float32)
    model_plane = jax.ops.segment_sum(blocks, cell_ids, num_segments=NF * NSEG)
    model_plane = jnp.transpose(model_plane.reshape(NF, NSEG, C, K), (2, 0, 1, 3))
    residual = tdi_data - model_plane
    weighted = apply_noise(residual, noise_diag, noise_off)
    summed = jnp.sum(residual * weighted)
    log_like = jnp.reshape(-0.5 * summed / (C * NF * NT), (1,)).astype(jnp.float32)
    flat_plane = jnp.transpose(weighted, (1, 2, 0, 3)).reshape(NF * NSEG, C, K)
    grad_blocks = jnp.take(flat_plane, cell_ids, axis=0).astype(jnp.bfloat16)
    return weighted, log_like, grad_blocks
```

```python
import functools

import jax
import jax.numpy as jnp
from jax import lax
from jax.experimental import pallas as pl
from jax.experimental.pallas import tpu as pltpu
from jax.sharding import PartitionSpec as P

LANES = 128
TAIL = 16
VMEM = pl.BlockSpec(memory_space=pltpu.VMEM)
HBM = pl.BlockSpec(memory_space=pltpu.HBM)
SMEM = pl.BlockSpec(memory_space=pltpu.SMEM)
F32 = jnp.float32
BF16 = jnp.bfloat16
I32 = jnp.int32


def passed_along(value, axis, steps):
    count = lax.axis_size(axis)
    leading, last = (max(0, -steps), min(count, count - steps))
    return lax.ppermute(value, axis, [(source, source + steps) for source in range(leading, last)])


def all_sum(value, axes):
    for axis in axes:
        count, step = lax.axis_size(axis), 1
        while step < count:
            value = value + lax.ppermute(value, axis, [(i, i ^ step) for i in range(count)])
            step *= 2
    return value


def halves_of(slots):
    return max(1, slots // LANES)


def pack_kernel(
    groups, slots, own_hbm, layer_hbm, seg_hbm, src_hbm, out_ref, pos_ref,
    own_ref, layer_ref, seg_ref, src_ref, sems,
):
    copies = [
        pltpu.make_async_copy(source, target, sems.at[i])
        for i, (source, target) in enumerate(
            ((own_hbm, own_ref), (layer_hbm, layer_ref), (seg_hbm, seg_ref), (src_hbm, src_ref))
        )
    ]
    for copy in copies:
        copy.start()
    copies[0].wait()
    count = own_ref.shape[1]
    own = own_ref[...]
    rows = max(16, groups)
    owned = (lax.broadcasted_iota(I32, (rows, count), 0) == own).astype(F32)
    width = min(count, 256)
    before = (
        lax.broadcasted_iota(I32, (width, width), 0) < lax.broadcasted_iota(I32, (width, width), 1)
    ).astype(F32).astype(BF16)
    carry = jnp.zeros((rows, 1), F32)
    ranks = []
    for start in range(0, count, width):
        part = owned[:, start : start + width]
        earlier = jnp.dot(part.astype(BF16), before, preferred_element_type=F32) + carry
        ranks.append(jnp.sum(part * earlier, axis=0, keepdims=True))
        carry = carry + jnp.sum(part, axis=1, keepdims=True)
    rank = jnp.concatenate(ranks, axis=1).astype(I32)
    pos_ref[...] = own * slots + rank
    tall = max(slots, LANES)
    for copy in copies[1:]:
        copy.wait()
    even = lax.broadcasted_iota(I32, (TAIL, count), 0) % 2 == 0
    names = jnp.where(even, layer_ref[...], seg_ref[...]).astype(F32).astype(BF16)
    slot = lax.broadcasted_iota(I32, (tall, count), 0)
    tail_row = lax.broadcasted_iota(I32, (TAIL, LANES), 0)

    def one(group, carried):
        key = jnp.where(own == group, rank, -1)
        chosen = (slot == key).astype(F32).astype(BF16)
        block = jnp.dot(chosen[:slots], src_ref[...], preferred_element_type=F32)
        cells = lax.dot_general(
            names, chosen, (((1,), (1,)), ((), ())), preferred_element_type=F32
        )
        tail = cells[:, :LANES]
        for half in range(1, halves_of(slots)):
            tail = jnp.where(
                tail_row < 2 * half, tail, cells[:, half * LANES : (half + 1) * LANES]
            )
        out_ref[group, :slots] = block.astype(BF16)
        out_ref[group, slots:] = tail.astype(BF16)
        return carried

    lax.fori_loop(0, groups, one, 0, unroll=groups <= 8)


def cells_of(arrived_ref, group, slots, segs):
    tail = arrived_ref[group, slots:].astype(F32)
    return [
        tail[2 * half : 2 * half + 1] * segs + tail[2 * half + 1 : 2 * half + 2]
        for half in range(halves_of(slots))
    ]


def rim_kernel(slots, layers, arrived_ref, low_ref, high_ref, off_ref, bottom_ref, prod_ref):
    groups = arrived_ref.shape[0]
    segs = low_ref.shape[0]
    line = lax.broadcasted_iota(I32, (2 * segs, LANES), 0)
    wanted = jnp.where(line < segs, line, line + (layers - 2) * segs).astype(F32)
    wide = min(slots, LANES)

    def one(group, total):
        for half, cells in enumerate(cells_of(arrived_ref, group, slots, segs)):
            chosen = (wanted == cells).astype(F32).astype(BF16)
            total = total + jnp.dot(
                chosen[:, :wide],
                arrived_ref[group, half * wide : (half + 1) * wide],
                preferred_element_type=F32,
            )
        return total

    model = lax.fori_loop(
        0, groups, one, jnp.zeros((2 * segs, LANES), F32), unroll=groups <= 8
    )
    bottom_ref[...] = low_ref[...] - model[:segs]
    prod_ref[...] = off_ref[...] * (high_ref[...] - model[segs:])


def scatter_kernel(
    slots, segs, arrived_ref, tdi_hbm, diag_hbm, off_hbm,
    resid_ref, extra_ref, diag_ref, off_ref, cell_ref, blocks, cells, sem, sems,
):
    copies = [
        pltpu.make_async_copy(source, target, sems.at[i])
        for i, (source, target) in enumerate(
            ((tdi_hbm, resid_ref), (diag_hbm, diag_ref), (off_hbm, off_ref))
        )
    ]
    for copy in copies:
        copy.start()
    groups = arrived_ref.shape[0]
    halves = halves_of(slots)
    wide = min(slots, LANES)

    def name(group, carried):
        for half, row in enumerate(cells_of(arrived_ref, group, slots, segs)):
            cell_ref[pl.ds(group * halves + half, 1), :] = row.astype(I32)
        return carried

    lax.fori_loop(0, groups, name, 0, unroll=groups <= 8)
    copy = pltpu.make_async_copy(cell_ref, cells, sem)
    copy.start()

    def widen(group, carried):
        blocks[pl.ds(pl.multiple_of(group * slots, slots), slots), :] = arrived_ref[
            group, :slots
        ].astype(F32)
        return carried

    lax.fori_loop(0, groups, widen, 0, unroll=groups <= 8)
    extra_ref[...] = jnp.zeros_like(extra_ref)
    copy.wait()
    copies[0].wait()

    def scatter(line, carried):
        for slot in range(0, wide, 2):
            for step, plane in enumerate((resid_ref, extra_ref)):
                place = pl.ds(cells[line, slot + step], 1)
                plane[place, :] = plane[place, :] - blocks[
                    pl.ds(line * wide + slot + step, 1), :
                ]
        return carried

    lax.fori_loop(0, groups * halves, scatter, 0)
    for copy in copies[1:]:
        copy.wait()


def weigh_kernel(
    slots, layers, chunk, resid_ref, extra_ref, diag_ref, off_ref, lower_ref, upper_ref, cells,
    weighted_ref, picked_ref, sum_ref, plane, sems,
):
    segs = lower_ref.shape[0]
    steps = layers // chunk
    size = chunk * segs

    def layer_rows(layer):
        return pl.ds(pl.multiple_of(layer * segs, segs), segs)

    def send(step):
        place = pl.ds(pl.multiple_of(step * size, size), size)
        return pltpu.make_async_copy(plane.at[place], weighted_ref.at[place], sems.at[step])

    def weigh(layer, carried):
        here, below, total = carried
        place, above_place = layer_rows(layer), layer_rows(layer + 1)
        above = resid_ref[above_place, :] + extra_ref[above_place, :]
        coupling = off_ref[place, :]
        out = diag_ref[place, :] * here + coupling * above + below
        plane[place, :] = out
        return above, coupling * here, total + here * out

    first, last = layer_rows(0), layer_rows(layers - 1)
    carried = (
        resid_ref[first, :] + extra_ref[first, :],
        lower_ref[...],
        jnp.zeros((segs, LANES), F32),
    )
    for step in range(steps):
        stop = min((step + 1) * chunk, layers - 1)
        carried = lax.fori_loop(step * chunk, stop, weigh, carried)
        if step < steps - 1:
            send(step).start()
    here, below, total = carried
    out = diag_ref[last, :] * here + off_ref[last, :] * upper_ref[...] + below
    plane[last, :] = out
    send(steps - 1).start()
    total = jnp.sum(total + here * out, axis=0, keepdims=True)
    sum_ref[...] = jnp.broadcast_to(jnp.sum(total, axis=1, keepdims=True), (1, LANES))
    wide = min(slots, LANES)

    def gather(line, carried):
        for slot in range(0, wide, 16):
            rows = [plane[pl.ds(cells[line, slot + step], 1), :] for step in range(16)]
            place = pl.ds(pl.multiple_of(line * wide + slot, 16), 16)
            picked_ref[place, :] = jnp.concatenate(rows, axis=0).astype(BF16)
        return carried

    lax.fori_loop(0, cells.shape[0], gather, 0)
    for step in range(steps):
        send(step).wait()


def unpack_kernel(slots, pos_ref, returned_ref, out_ref):
    groups = returned_ref.shape[0]
    count = pos_ref.shape[1]
    wide = min(slots, LANES)
    pos = jnp.transpose(jnp.broadcast_to(pos_ref[...], (LANES, count)).astype(F32))
    lane = lax.broadcasted_iota(I32, (count, LANES), 1).astype(F32)

    def one(group, total):
        for start in range(0, slots, wide):
            base = (group * slots + start) * jnp.float32(1)
            chosen = (pos - base == lane).astype(F32).astype(BF16)
            total = total + jnp.dot(
                chosen[:, :wide],
                returned_ref[group, start : start + wide],
                preferred_element_type=F32,
            )
        return total

    total = lax.fori_loop(0, groups, one, jnp.zeros((count, LANES), F32), unroll=groups <= 8)
    out_ref[...] = total.astype(BF16)


def in_hbm(*arrays):
    return [pltpu.with_memory_space_constraint(array, pltpu.HBM) for array in arrays]


def shape_of(shape, dtype):
    return jax.ShapeDtypeStruct(shape, dtype)


def params(mib):
    return pltpu.CompilerParams(vmem_limit_bytes=mib << 20)


def shards(tdi_data, noise_diag, noise_off, src_blocks, owner_dev, layer_in, seg_in):
    axes = ("band", "tm")
    groups = lax.axis_size("band") * lax.axis_size("tm")
    _, layers, segs, bins = tdi_data.shape
    count = src_blocks.shape[0]
    slots = 2 * count // groups
    block = slots + TAIL
    lines = groups * halves_of(slots)
    cell_count = layers * segs
    tdi = tdi_data.reshape(cell_count, bins)
    diag = noise_diag.reshape(cell_count, bins)
    off = noise_off.reshape(cell_count, bins)
    outgoing, position = pl.pallas_call(
        functools.partial(pack_kernel, groups, slots),
        out_shape=(shape_of((groups, block, bins), BF16), shape_of((1, count), I32)),
        in_specs=[HBM] * 4,
        out_specs=(VMEM, VMEM),
        scratch_shapes=[
            pltpu.VMEM((1, count), I32),
            pltpu.VMEM((1, count), I32),
            pltpu.VMEM((1, count), I32),
            pltpu.VMEM((count, bins), BF16),
            pltpu.SemaphoreType.DMA((4,)),
        ],
        compiler_params=params(48),
    )(
        *in_hbm(
            owner_dev.reshape(1, count),
            layer_in.reshape(1, count),
            seg_in.reshape(1, count),
            src_blocks.reshape(count, bins),
        )
    )
    arrived = lax.all_to_all(outgoing, axes, split_axis=0, concat_axis=0, tiled=True)
    rim = shape_of((segs, bins), F32)
    bottom, product = pl.pallas_call(
        functools.partial(rim_kernel, slots, layers),
        out_shape=(rim, rim),
        in_specs=[VMEM] * 4,
        out_specs=(VMEM, VMEM),
        compiler_params=params(16),
    )(arrived, tdi[:segs], tdi[-segs:], off[-segs:])
    lower_rim = passed_along(product, "band", 1)
    upper_rim = passed_along(bottom, "band", -1)
    plane = shape_of((cell_count, bins), F32)
    resid, extra, diag, off, cells = pl.pallas_call(
        functools.partial(scatter_kernel, slots, segs),
        out_shape=(plane,) * 4 + (shape_of((lines, LANES), I32),),
        in_specs=[VMEM] + [HBM] * 3,
        out_specs=(VMEM,) * 5,
        scratch_shapes=[
            pltpu.VMEM((groups * slots, bins), F32),
            pltpu.SMEM((lines, LANES), I32),
            pltpu.SemaphoreType.DMA,
            pltpu.SemaphoreType.DMA((3,)),
        ],
        compiler_params=params(24),
    )(arrived, *in_hbm(tdi, diag, off))
    chunk = max(1, layers // 8)
    weighted, picked, summed = pl.pallas_call(
        functools.partial(weigh_kernel, slots, layers, chunk),
        out_shape=(plane, shape_of((groups * slots, bins), BF16), shape_of((1, bins), F32)),
        in_specs=[VMEM] * 6 + [SMEM],
        out_specs=(HBM, VMEM, VMEM),
        scratch_shapes=[
            pltpu.VMEM((cell_count, bins), F32),
            pltpu.SemaphoreType.DMA((layers // chunk,)),
        ],
        compiler_params=params(24),
    )(resid, extra, diag, off, lower_rim, upper_rim, cells)
    returned = lax.all_to_all(
        picked.reshape(groups, slots, bins), axes, split_axis=0, concat_axis=0, tiled=True
    )
    summed = all_sum(summed, ("chan", "tm", "band"))
    cells_all = lax.axis_size("chan") * groups * cell_count * bins
    log_like = -0.5 * summed[0, :1] / cells_all
    grads = pl.pallas_call(
        functools.partial(unpack_kernel, slots),
        out_shape=shape_of((count, bins), BF16),
        in_specs=[VMEM, VMEM],
        out_specs=VMEM,
        compiler_params=params(16),
    )(position, returned)
    return (
        weighted.reshape(tdi_data.shape),
        log_like,
        grads.reshape(src_blocks.shape),
    )


def solution(mesh):
    planes = P(("grp", "chan"), "band", "tm", None)
    lists = P(("grp", "band", "tm"))
    return jax.shard_map(
        shards,
        mesh=mesh,
        in_specs=(
            planes,
            planes,
            planes,
            P(("grp", "band", "tm"), "chan", None),
            P(("grp", "band", "tm"), None),
            lists,
            lists,
        ),
        out_specs=(planes, P("grp"), P(("grp", "band", "tm"), "chan", None)),
        check_vma=False,
    )
```

```python
import functools

import jax
import jax.numpy as jnp
from jax import lax
from jax.experimental import pallas as pl
from jax.experimental.pallas import tpu as pltpu
from jax.sharding import PartitionSpec as P

LANES = 128
TAIL = 16
AXES = ("band", "tm")
VMEM = pl.BlockSpec(memory_space=pltpu.VMEM)
SMEM = pl.BlockSpec(memory_space=pltpu.SMEM)
HBM = pl.BlockSpec(memory_space=pltpu.HBM)
HBM_BYTES_PER_US = 3_300_000
F32 = jnp.float32
BF16 = jnp.bfloat16
I32 = jnp.int32


def passed_along(value, axis, steps):
    count = lax.axis_size(axis)
    leading, last = (max(0, -steps), min(count, count - steps))
    return lax.ppermute(value, axis, [(source, source + steps) for source in range(leading, last)])


def halves_of(slots):
    return max(1, slots // LANES)


def few(count):
    return count <= 8


def each(refs, firsts, body, carried=0):
    if firsts is None:
        firsts = [sum(ref.shape[0] for ref in refs[:i]) for i in range(len(refs))]
    for ref, first in zip(refs, firsts):
        length = ref.shape[0]
        carried = lax.fori_loop(
            0,
            length,
            lambda i, value, ref=ref, first=first: body(ref, i, first + i, value),
            carried,
            unroll=few(length),
        )
    return carried


def pack_blocks(slots, firsts, pos, names, src_ref, outs):
    count = pos.shape[1]
    slot = lax.broadcasted_iota(I32, (max(slots, LANES), count), 0)
    tail_row = lax.broadcasted_iota(I32, (TAIL, LANES), 0)

    def one(ref, i, block, carried):
        chosen = (slot == pos - block * slots).astype(F32).astype(BF16)
        if slots < LANES:
            chosen = jnp.where(slot < slots, chosen, jnp.zeros_like(chosen))
        rows = jnp.dot(chosen[:slots], src_ref[...], preferred_element_type=F32)
        cells = lax.dot_general(
            names, chosen, (((1,), (1,)), ((), ())), preferred_element_type=F32
        )
        tail = cells[:, :LANES]
        for half in range(1, halves_of(slots)):
            tail = jnp.where(
                tail_row < 2 * half, tail, cells[:, half * LANES : (half + 1) * LANES]
            )
        ref[i, :slots] = rows.astype(BF16)
        ref[i, slots:] = tail.astype(BF16)
        return carried

    each(outs, firsts, one)


def pack_kernel(
    slots, groups, direct, firsts, own_hbm, layer_hbm, seg_hbm, src_hbm,
    pos_ref, names_ref, src_ref, *rest,
):
    outs, (own_ref, layer_ref, seg_ref, sems) = rest[:-4], rest[-4:]
    copies = [
        pltpu.make_async_copy(source, target, sems.at[i])
        for i, (source, target) in enumerate(
            ((own_hbm, own_ref), (layer_hbm, layer_ref), (seg_hbm, seg_ref), (src_hbm, src_ref))
        )
    ]
    for copy in copies:
        copy.start()
    count = own_ref.shape[1]
    width = min(count, 256)
    before = (
        lax.broadcasted_iota(I32, (width, width), 0) < lax.broadcasted_iota(I32, (width, width), 1)
    ).astype(F32).astype(BF16)
    copies[0].wait()
    own = own_ref[...]
    if direct:
        own = own ^ (lax.axis_index("band") * lax.axis_size("tm") + lax.axis_index("tm"))
    rows = max(16, groups)
    owned = (lax.broadcasted_iota(I32, (rows, count), 0) == own).astype(F32)
    carry = jnp.zeros((rows, 1), F32)
    ranks = []
    for start in range(0, count, width):
        part = owned[:, start : start + width]
        earlier = jnp.dot(part.astype(BF16), before, preferred_element_type=F32) + carry
        ranks.append(jnp.sum(part * earlier, axis=0, keepdims=True))
        carry = carry + jnp.sum(part, axis=1, keepdims=True)
    pos = own * slots + jnp.concatenate(ranks, axis=1).astype(I32)
    pos_ref[...] = pos
    for copy in copies[1:]:
        copy.wait()
    even = lax.broadcasted_iota(I32, (TAIL, count), 0) % 2 == 0
    names = jnp.where(even, layer_ref[...], seg_ref[...]).astype(F32).astype(BF16)
    names_ref[...] = names
    pack_blocks(slots, firsts, pos, names, src_ref, outs)


def repack_kernel(slots, firsts, after_ref, pos_ref, names_ref, src_ref, *outs):
    pack_blocks(slots, firsts, pos_ref[...], names_ref[...], src_ref, outs)


def cells_of(ref, i, slots, segs):
    tail = ref[i, slots:].astype(F32)
    return [
        tail[2 * half : 2 * half + 1] * segs + tail[2 * half + 1 : 2 * half + 2]
        for half in range(halves_of(slots))
    ]


def rim_kernel(slots, layers, low_ref, high_ref, off_ref, *rest):
    chunks, (bottom_ref, prod_ref) = rest[:-2], rest[-2:]
    segs = low_ref.shape[0]
    line = lax.broadcasted_iota(I32, (2 * segs, LANES), 0)
    wanted = jnp.where(line < segs, line, line + (layers - 2) * segs).astype(F32)
    wide = min(slots, LANES)

    def one(ref, i, block, total):
        for half, cells in enumerate(cells_of(ref, i, slots, segs)):
            chosen = (wanted == cells).astype(F32).astype(BF16)
            total = total + jnp.dot(
                chosen[:, :wide],
                ref[i, half * wide : (half + 1) * wide],
                preferred_element_type=F32,
            )
        return total

    model = each(chunks, None, one, jnp.zeros((2 * segs, LANES), F32))
    bottom_ref[...] = low_ref[...] - model[:segs]
    prod_ref[...] = off_ref[...] * (high_ref[...] - model[segs:])


def scatter_blocks(slots, segs, chunks, resid_ref, extra_ref, cell_ref, blocks, cells, sem, ready):
    halves = halves_of(slots)
    wide = min(slots, LANES)

    def name(ref, i, block, carried):
        for half, row in enumerate(cells_of(ref, i, slots, segs)):
            cell_ref[pl.ds(block * halves + half, 1), :] = row.astype(I32)
        return carried

    each(chunks, None, name)
    copy = pltpu.make_async_copy(cell_ref, cells, sem)
    copy.start()

    def widen(ref, i, block, carried):
        blocks[pl.ds(pl.multiple_of(block * slots, slots), slots), :] = ref[i, :slots].astype(F32)
        return carried

    each(chunks, None, widen)
    ready()
    copy.wait()

    def scatter(line, carried):
        for slot in range(0, wide, 2):
            for step, plane in enumerate((resid_ref, extra_ref)):
                place = pl.ds(cells[line, slot + step], 1)
                plane[place, :] = plane[place, :] - blocks[
                    pl.ds(line * wide + slot + step, 1), :
                ]
        return carried

    lax.fori_loop(0, cell_ref.shape[0], scatter, 0)


def first_scatter_kernel(slots, segs, tdi_hbm, diag_hbm, off_hbm, *rest):
    chunks, outs, (blocks, cells, sem, sems) = rest[:-12], rest[-12:-4], rest[-4:]
    resid_ref, extra_ref, diag_ref, off_ref, low_ref, high_ref, last_ref, cell_ref = outs
    size = resid_ref.shape[0]
    copies = [
        pltpu.make_async_copy(source, target, sems.at[i])
        for i, (source, target) in enumerate(
            ((tdi_hbm, resid_ref), (diag_hbm, diag_ref), (off_hbm, off_ref))
        )
    ]
    for copy in copies:
        copy.start()

    def ready():
        extra_ref[...] = jnp.zeros_like(extra_ref)
        copies[0].wait()
        low_ref[...] = resid_ref[:segs]
        high_ref[...] = resid_ref[size - segs :]

    scatter_blocks(slots, segs, chunks, resid_ref, extra_ref, cell_ref, blocks, cells, sem, ready)
    for copy in copies[1:]:
        copy.wait()
    last_ref[...] = off_ref[size - segs :]


def scatter_kernel(slots, segs, resid_in, extra_in, *rest):
    chunks, (resid_ref, extra_ref, cell_ref, blocks, cells, sem) = rest[:-6], rest[-6:]
    scatter_blocks(
        slots, segs, chunks, resid_ref, extra_ref, cell_ref, blocks, cells, sem, lambda: None
    )


def weigh_kernel(segs, layers, resid_ref, extra_ref, diag_ref, off_ref, plane_ref, part_ref):
    def layer_rows(layer):
        return pl.ds(pl.multiple_of(layer * segs, segs), segs)

    def weigh(layer, carried):
        here, below, total = carried
        place, above_place = layer_rows(layer), layer_rows(layer + 1)
        above = resid_ref[above_place, :] + extra_ref[above_place, :]
        coupling = off_ref[place, :]
        out = diag_ref[place, :] * here + coupling * above + below
        plane_ref[place, :] = out
        return above, coupling * here, total + here * out

    first, last = layer_rows(0), layer_rows(layers - 1)
    zero = jnp.zeros((segs, LANES), F32)
    here, below, total = lax.fori_loop(
        0, layers - 1, weigh, (resid_ref[first, :] + extra_ref[first, :], zero, zero), unroll=4
    )
    out = diag_ref[last, :] * here + below
    plane_ref[last, :] = out
    part_ref[...] = jnp.sum(total + here * out, axis=0, keepdims=True)


def gather_blocks(slots, plane_ref, cell_refs, outs):
    halves = halves_of(slots)
    wide = min(slots, LANES)

    for cells, out in zip(cell_refs, outs):

        def gather(line, carried, cells=cells, out=out):
            block, half = line // halves, line % halves
            for slot in range(0, wide, 16):
                rows = [plane_ref[pl.ds(cells[line, slot + step], 1), :] for step in range(16)]
                place = pl.ds(pl.multiple_of(half * wide + slot, 16), 16)
                out[block, place, :] = jnp.concatenate(rows, axis=0).astype(BF16)
            return carried

        lax.fori_loop(0, cells.shape[0], gather, 0)


def put_sum(slots, total, outs):
    high = total.astype(BF16).astype(F32)
    middle = (total - high).astype(BF16).astype(F32)
    low = total - high - middle
    row = lax.broadcasted_iota(I32, (TAIL, LANES), 0)
    tail = jnp.where(row == 0, high, jnp.where(row == 1, middle, jnp.where(row == 2, low, 0.0)))

    def one(ref, i, block, carried):
        ref[i, slots:] = tail.astype(BF16)
        return carried

    each(outs, None, one)


def pick_kernel(
    slots, chunks, plane_in, part_ref, lower_ref, upper_ref, off_ref, bottom_ref, prod_ref, *rest
):
    cell_refs = rest[:chunks]
    plane_ref, sum_ref = rest[chunks : chunks + 2]
    outs = rest[chunks + 2 :]
    segs = lower_ref.shape[0]
    first, last = pl.ds(0, segs), pl.ds(plane_ref.shape[0] - segs, segs)
    plane_ref[first, :] = plane_ref[first, :] + lower_ref[...]
    plane_ref[last, :] = plane_ref[last, :] + off_ref[...] * upper_ref[...]
    rims = bottom_ref[...] * lower_ref[...] + prod_ref[...] * upper_ref[...]
    total = jnp.sum(part_ref[...] + jnp.sum(rims, axis=0, keepdims=True), axis=1, keepdims=True)
    total = jnp.broadcast_to(total, (1, LANES))
    sum_ref[...] = total
    put_sum(slots, total, outs)
    gather_blocks(slots, plane_ref, cell_refs, outs)


def repick_kernel(slots, chunks, plane_ref, sum_ref, *rest):
    cell_refs, weighted_ref, outs, sem = rest[:chunks], rest[chunks], rest[chunks + 1 : -1], rest[-1]
    copy = pltpu.make_async_copy(plane_ref, weighted_ref, sem)
    copy.start()
    put_sum(slots, sum_ref[...], outs)
    gather_blocks(slots, plane_ref, cell_refs, outs)
    copy.wait()


def unpacked(slots, firsts, pos, chunks, total):
    lane = lax.broadcasted_iota(I32, pos.shape, 1).astype(F32)
    wide = min(slots, LANES)

    def one(ref, i, block, total):
        for start in range(0, slots, wide):
            base = jnp.asarray(block * slots + start, I32).astype(F32)
            chosen = (pos - base == lane).astype(F32).astype(BF16)
            total = total + jnp.dot(
                chosen[:, :wide], ref[i, start : start + wide], preferred_element_type=F32
            )
        return total

    return each(chunks, firsts, one, total)


def unpack_kernel(slots, firsts, pos_ref, *rest):
    chunks, (places_ref, total_ref) = rest[:-2], rest[-2:]
    count = pos_ref.shape[1]
    pos = jnp.transpose(jnp.broadcast_to(pos_ref[...], (LANES, count)).astype(F32))
    places_ref[...] = pos
    total_ref[...] = unpacked(slots, firsts, pos, chunks, jnp.zeros((count, LANES), F32))


def last_unpack_kernel(slots, firsts, places_ref, total_ref, *rest):
    chunks, out_ref = rest[:-1], rest[-1]
    out_ref[...] = unpacked(slots, firsts, places_ref[...], chunks, total_ref[...]).astype(BF16)


def sum_kernel(slots, after_ref, *rest):
    chunks, out_ref = rest[:-1], rest[-1]

    def one(ref, i, block, total):
        tail = ref[i, slots:].astype(F32)
        return total + tail[0:1] + tail[1:2] + tail[2:3]

    out_ref[...] = each(chunks, None, one, jnp.zeros((1, LANES), F32))


def shape_of(shape, dtype):
    return jax.ShapeDtypeStruct(shape, dtype)


def params(mib):
    return pltpu.CompilerParams(vmem_limit_bytes=mib << 20)


def in_hbm(*arrays):
    return [pltpu.with_memory_space_constraint(array, pltpu.HBM) for array in arrays]


def call(kernel, args, in_specs, out_shape, out_specs, scratch=(), aliases=None, us=1.0):
    return pl.pallas_call(
        kernel,
        out_shape=tuple(out_shape),
        in_specs=list(in_specs),
        out_specs=tuple(out_specs),
        scratch_shapes=list(scratch),
        input_output_aliases=aliases or {},
        compiler_params=params(8),
        cost_estimate=pl.CostEstimate(
            flops=0, bytes_accessed=int(us * HBM_BYTES_PER_US), transcendentals=0
        ),
    )(*args)


def shards(tdi_data, noise_diag, noise_off, src_blocks, owner_dev, layer_in, seg_in):
    groups = lax.axis_size("band") * lax.axis_size("tm")
    _, layers, segs, bins = tdi_data.shape
    count = src_blocks.shape[0]
    slots = 2 * count // groups
    halves = halves_of(slots)
    cell_count = layers * segs
    direct = groups == 8
    if direct:
        sizes, first_out, second_out = [1] * groups, [7, 6, 5, 4, 3, 2, 1, 0], []
        first_back, second_back = [7, 6, 5, 4, 3, 2, 1], [0]
        first_in, second_in = [0, 7, 6], [5, 4, 3, 2, 1]
        early, late = [0, 7, 6, 5, 4, 3], [2, 1]
    else:
        sizes, first_out, second_out = [groups], [0], []
        first_back, second_back = [0], []
        first_in, second_in = [0], []
        early, late = [], [0]
    total = len(sizes)

    def exchanged(number, block):
        if not direct:
            return lax.all_to_all(block, AXES, split_axis=0, concat_axis=0, tiled=True)
        if number == 0:
            return block
        return lax.ppermute(block, AXES, [(i, i ^ number) for i in range(groups)])

    blocks = [shape_of((size, slots + TAIL, bins), BF16) for size in sizes]
    plane = pltpu.VMEM((cell_count, bins), F32)
    rim = shape_of((segs, bins), F32)
    line = shape_of((1, bins), F32)
    tdi = tdi_data.reshape(cell_count, bins)
    diag = noise_diag.reshape(cell_count, bins)
    off = noise_off.reshape(cell_count, bins)

    arrived = [None] * total
    pos, names, src, *packed = call(
        functools.partial(pack_kernel, slots, groups, direct, first_out),
        in_hbm(
            owner_dev.reshape(1, count),
            layer_in.reshape(1, count),
            seg_in.reshape(1, count),
            src_blocks.reshape(count, bins),
        ),
        [HBM] * 4,
        [
            pltpu.VMEM((1, count), I32),
            pltpu.VMEM((TAIL, count), BF16),
            pltpu.VMEM((count, bins), BF16),
        ]
        + [blocks[k] for k in first_out],
        [VMEM] * (3 + len(first_out)),
        [pltpu.VMEM((1, count), I32)] * 3 + [pltpu.SemaphoreType.DMA((4,))],
        us=2.5,
    )
    for k, block in zip(first_out, packed):
        arrived[k] = exchanged(k, block)
    if second_out:
        packed = call(
            functools.partial(repack_kernel, slots, second_out),
            (arrived[first_out[0]], pos, names, src),
            [VMEM] * 4,
            [blocks[k] for k in second_out],
            [VMEM] * len(second_out),
        )
        for k, block in zip(second_out, packed):
            arrived[k] = exchanged(k, block)

    cells = [None] * total

    def scratch_of(step):
        size = sum(sizes[k] for k in step)
        return [
            pltpu.VMEM((size * slots, bins), F32),
            pltpu.SMEM((size * halves, LANES), I32),
            pltpu.SemaphoreType.DMA,
        ]

    def lines_of(step):
        return shape_of((sum(sizes[k] for k in step) * halves, LANES), I32)

    def split_lines(step, joined):
        start = 0
        for k in step:
            stop = start + sizes[k] * halves
            cells[k] = joined[start:stop]
            start = stop

    resid, extra, diag_in, off_in, low, high, off_last, joined = call(
        functools.partial(first_scatter_kernel, slots, segs),
        in_hbm(tdi, diag, off) + [arrived[k] for k in first_in],
        [HBM] * 3 + [VMEM] * len(first_in),
        [plane] * 4 + [rim] * 3 + [lines_of(first_in)],
        [VMEM] * 8,
        scratch_of(first_in) + [pltpu.SemaphoreType.DMA((3,))],
        us=5.0,
    )
    split_lines(first_in, joined)
    bottom, product = call(
        functools.partial(rim_kernel, slots, layers),
        (low, high, off_last, *arrived),
        [VMEM] * (3 + total),
        (rim, rim),
        (VMEM, VMEM),
        us=0.3,
    )
    lower_rim = passed_along(product, "band", 1)
    upper_rim = passed_along(bottom, "band", -1)
    if second_in:
        resid, extra, joined = call(
            functools.partial(scatter_kernel, slots, segs),
            [resid, extra] + [arrived[k] for k in second_in],
            [VMEM] * (2 + len(second_in)),
            [plane] * 2 + [lines_of(second_in)],
            [VMEM] * 3,
            scratch_of(second_in),
            {0: 0, 1: 1},
            us=4.0,
        )
        split_lines(second_in, joined)
    weighed, part = call(
        functools.partial(weigh_kernel, segs, layers),
        (resid, extra, diag_in, off_in),
        [VMEM] * 4,
        (plane, line),
        (VMEM, VMEM),
        us=2.4,
    )
    returned = [None] * total
    weighed, summed, *picked = call(
        functools.partial(pick_kernel, slots, len(first_back)),
        (weighed, part, lower_rim, upper_rim, off_last, bottom, product)
        + tuple(cells[k] for k in first_back),
        [VMEM] * 7 + [SMEM] * len(first_back),
        [plane, line] + [blocks[k] for k in first_back],
        [VMEM] * (2 + len(first_back)),
        aliases={0: 0},
        us=1.7,
    )
    for k, block in zip(first_back, picked):
        returned[k] = exchanged(k, block)
    weighted, *picked = call(
        functools.partial(repick_kernel, slots, len(second_back)),
        (weighed, summed)
        + tuple(cells[k] for k in second_back),
        [VMEM] * 2 + [SMEM] * len(second_back),
        [shape_of((cell_count, bins), F32)] + [blocks[k] for k in second_back],
        [HBM] + [VMEM] * len(second_back),
        [pltpu.SemaphoreType.DMA],
        us=2.0,
    )
    for k, block in zip(second_back, picked):
        returned[k] = exchanged(k, block)

    places, grads = call(
        functools.partial(unpack_kernel, slots, early),
        [pos] + [returned[k] for k in early],
        [VMEM] * (1 + len(early)),
        [pltpu.VMEM((count, LANES), F32)] * 2,
        (VMEM, VMEM),
    )
    (total_sum,) = call(
        functools.partial(sum_kernel, slots),
        [places] + returned,
        [VMEM] * (1 + total),
        (line,),
        (VMEM,),
        us=0.1,
    )
    chan = lax.axis_size("chan")
    other_sum = lax.ppermute(total_sum, "chan", [(i, i ^ 1) for i in range(chan)])
    cells_all = chan * groups * cell_count * bins
    log_like = (total_sum + other_sum)[0, :1] * (-0.5 / cells_all)
    (grads,) = call(
        functools.partial(last_unpack_kernel, slots, late),
        [places, grads] + [returned[k] for k in late],
        [VMEM] * (2 + len(late)),
        (shape_of((count, bins), BF16),),
        (VMEM,),
    )
    return (
        weighted.reshape(tdi_data.shape),
        log_like,
        grads.reshape(src_blocks.shape),
    )


def solution(mesh):
    planes = P(("grp", "chan"), "band", "tm", None)
    lists = P(("grp", "band", "tm"))
    return jax.shard_map(
        shards,
        mesh=mesh,
        in_specs=(
            planes,
            planes,
            planes,
            P(("grp", "band", "tm"), "chan", None),
            P(("grp", "band", "tm"), None),
            lists,
            lists,
        ),
        out_specs=(planes, P("grp"), P(("grp", "band", "tm"), "chan", None)),
        check_vma=False,
    )
```

```python
import functools

import jax
import jax.numpy as jnp
from jax import lax
from jax.experimental import pallas as pl
from jax.experimental.pallas import tpu as pltpu
from jax.sharding import PartitionSpec as P

LANES = 128
TAIL = 16
AXES = ("band", "tm")
VMEM = pl.BlockSpec(memory_space=pltpu.VMEM)
SMEM = pl.BlockSpec(memory_space=pltpu.SMEM)
HBM = pl.BlockSpec(memory_space=pltpu.HBM)
HBM_BYTES_PER_US = 3_300_000
F32 = jnp.float32
BF16 = jnp.bfloat16
I32 = jnp.int32


def passed_along(value, axis, steps):
    count = lax.axis_size(axis)
    leading, last = (max(0, -steps), min(count, count - steps))
    return lax.ppermute(value, axis, [(source, source + steps) for source in range(leading, last)])


def halves_of(slots):
    return max(1, slots // LANES)


def few(count):
    return count <= 8


def each(refs, firsts, body, carried=0):
    if firsts is None:
        firsts = [sum(ref.shape[0] for ref in refs[:i]) for i in range(len(refs))]
    for ref, first in zip(refs, firsts):
        length = ref.shape[0]
        carried = lax.fori_loop(
            0,
            length,
            lambda i, value, ref=ref, first=first: body(ref, i, first + i, value),
            carried,
            unroll=few(length),
        )
    return carried


def pack_kernel(
    slots, groups, direct, firsts, own_hbm, layer_hbm, seg_hbm, src_hbm, pos_ref, *rest
):
    outs, (own_ref, layer_ref, seg_ref, wide_ref, sems) = rest[:-5], rest[-5:]
    src_ref = wide_ref.at[:, pl.ds(0, LANES)]
    copies = [
        pltpu.make_async_copy(source, target, sems.at[i])
        for i, (source, target) in enumerate(
            ((own_hbm, own_ref), (layer_hbm, layer_ref), (seg_hbm, seg_ref), (src_hbm, src_ref))
        )
    ]
    for copy in copies:
        copy.start()
    count = own_ref.shape[1]
    width = min(count, 256)
    before = (
        lax.broadcasted_iota(I32, (width, width), 0) < lax.broadcasted_iota(I32, (width, width), 1)
    ).astype(F32).astype(BF16)
    copies[0].wait()
    own = own_ref[...]
    if direct:
        own = own ^ (lax.axis_index("band") * lax.axis_size("tm") + lax.axis_index("tm"))
    rows = max(16, groups)
    owned = (lax.broadcasted_iota(I32, (rows, count), 0) == own).astype(F32)
    carry = jnp.zeros((rows, 1), F32)
    ranks = []
    for start in range(0, count, width):
        part = owned[:, start : start + width]
        earlier = jnp.dot(part.astype(BF16), before, preferred_element_type=F32) + carry
        ranks.append(jnp.sum(part * earlier, axis=0, keepdims=True))
        carry = carry + jnp.sum(part, axis=1, keepdims=True)
    pos = own * slots + jnp.concatenate(ranks, axis=1).astype(I32)
    pos_ref[...] = pos
    copies[1].wait()
    copies[2].wait()
    even = lax.broadcasted_iota(I32, (LANES, count), 0) % 2 == 0
    names = jnp.where(even, layer_ref[...], seg_ref[...]).astype(F32)
    wide_ref[:, LANES:] = jnp.transpose(names).astype(BF16)
    copies[3].wait()
    tall = max(slots, LANES)
    slot = lax.broadcasted_iota(I32, (tall, count), 0)
    lane_pair = lax.broadcasted_iota(I32, (tall, LANES), 1) // 2
    tail_row = lax.broadcasted_iota(I32, (TAIL, LANES), 0)

    def tail_of(named, row):
        tail = jnp.zeros((TAIL, LANES), F32)
        for half in range(halves_of(slots)):
            pair = named[row : row + 2, half * LANES : (half + 1) * LANES]
            for i in range(2):
                tail = jnp.where(tail_row == 2 * half + i, pair[i : i + 1], tail)
        return tail.astype(BF16)

    def one(ref, i, block, named):
        chosen = (slot == pos - block * slots).astype(F32).astype(BF16)
        if slots < LANES:
            chosen = jnp.where(slot < slots, chosen, jnp.zeros_like(chosen))
        found = jnp.dot(chosen, wide_ref[...], preferred_element_type=F32)
        ref[i, :slots] = found[:slots, :LANES].astype(BF16)
        if few(groups):
            return jnp.where(lane_pair == block, found[:, LANES:], named)
        ref[i, slots:] = tail_of(jnp.transpose(found[:, LANES:]), 0)
        return named

    named = each(outs, firsts, one, jnp.zeros((tall, LANES), F32))
    if few(groups):
        named = jnp.transpose(named)
        for ref, first in zip(outs, firsts):
            for i in range(ref.shape[0]):
                ref[i, slots:] = tail_of(named, 2 * (first + i))


def cells_of(ref, i, slots, segs):
    tail = ref[i, slots:].astype(F32)
    return [
        tail[2 * half : 2 * half + 1] * segs + tail[2 * half + 1 : 2 * half + 2]
        for half in range(halves_of(slots))
    ]


def rim_kernel(slots, layers, low_ref, high_ref, off_ref, *rest):
    chunks, (bottom_ref, prod_ref) = rest[:-2], rest[-2:]
    segs = low_ref.shape[0]
    line = lax.broadcasted_iota(I32, (2 * segs, LANES), 0)
    wanted = jnp.where(line < segs, line, line + (layers - 2) * segs).astype(F32)
    wide = min(slots, LANES)

    def one(ref, i, block, total):
        for half, cells in enumerate(cells_of(ref, i, slots, segs)):
            chosen = (wanted == cells).astype(F32).astype(BF16)
            total = total + jnp.dot(
                chosen[:, :wide],
                ref[i, half * wide : (half + 1) * wide],
                preferred_element_type=F32,
            )
        return total

    model = each(chunks, None, one, jnp.zeros((2 * segs, LANES), F32))
    bottom_ref[...] = low_ref[...] - model[:segs]
    prod_ref[...] = off_ref[...] * (high_ref[...] - model[segs:])


def scatter_blocks(slots, segs, chunks, resid_ref, extra_ref, cell_ref, blocks, cells, sem, ready):
    halves = halves_of(slots)
    wide = min(slots, LANES)

    def name(ref, i, block, carried):
        for half, row in enumerate(cells_of(ref, i, slots, segs)):
            cell_ref[pl.ds(block * halves + half, 1), :] = row.astype(I32)
        return carried

    each(chunks, None, name)
    copy = pltpu.make_async_copy(cell_ref, cells, sem)
    copy.start()

    def widen(ref, i, block, carried):
        blocks[pl.ds(pl.multiple_of(block * slots, slots), slots), :] = ref[i, :slots].astype(F32)
        return carried

    each(chunks, None, widen)
    ready()
    copy.wait()

    def scatter(line, carried):
        for slot in range(0, wide, 4):
            turns = []
            for step, plane in enumerate((resid_ref, extra_ref)):
                one, two = cells[line, slot + step], cells[line, slot + step + 2]
                first = blocks[pl.ds(line * wide + slot + step, 1), :]
                second = blocks[pl.ds(line * wide + slot + step + 2, 1), :]
                second = second + jnp.where(one == two, first, 0.0)
                one, two = pl.ds(one, 1), pl.ds(two, 1)
                turns.append((plane, one, two, plane[one, :] - first, plane[two, :] - second))
            for plane, one, two, first, second in turns:
                plane[one, :] = first
                plane[two, :] = second
        return carried

    lax.fori_loop(0, cell_ref.shape[0], scatter, 0)


def first_scatter_kernel(slots, segs, tdi_hbm, off_hbm, *rest):
    chunks, outs, (blocks, cells, sem, sems) = rest[:-10], rest[-10:-4], rest[-4:]
    resid_ref, extra_ref, low_ref, high_ref, last_ref, cell_ref = outs
    size = resid_ref.shape[0]
    copy = pltpu.make_async_copy(tdi_hbm, resid_ref, sems.at[0])
    copy_last = pltpu.make_async_copy(off_hbm.at[pl.ds(size - segs, segs)], last_ref, sems.at[1])
    copy_last.start()
    copy.start()

    def ready():
        extra_ref[...] = jnp.zeros_like(extra_ref)
        copy_last.wait()
        copy.wait()
        low_ref[...] = resid_ref[:segs]
        high_ref[...] = resid_ref[size - segs :]

    scatter_blocks(slots, segs, chunks, resid_ref, extra_ref, cell_ref, blocks, cells, sem, ready)


def scatter_kernel(slots, segs, resid_in, extra_in, diag_hbm, off_hbm, *rest):
    chunks, outs, (blocks, cells, sem, sems) = rest[:-9], rest[-9:-4], rest[-4:]
    resid_ref, extra_ref, diag_ref, off_ref, cell_ref = outs
    copies = [
        pltpu.make_async_copy(diag_hbm, diag_ref, sems.at[0]),
        pltpu.make_async_copy(off_hbm, off_ref, sems.at[1]),
    ]
    for copy in copies:
        copy.start()
    if chunks:
        scatter_blocks(
            slots, segs, chunks, resid_ref, extra_ref, cell_ref, blocks, cells, sem, lambda: None
        )
    for copy in copies:
        copy.wait()


def weigh_kernel(segs, layers, resid_ref, extra_ref, diag_ref, off_ref, plane_ref, part_ref):
    def layer_rows(layer):
        return pl.ds(pl.multiple_of(layer * segs, segs), segs)

    def weigh(layer, carried):
        here, below, total = carried
        place, above_place = layer_rows(layer), layer_rows(layer + 1)
        above = resid_ref[above_place, :] + extra_ref[above_place, :]
        coupling = off_ref[place, :]
        out = diag_ref[place, :] * here + coupling * above + below
        plane_ref[place, :] = out
        return above, coupling * here, total + here * out

    first, last = layer_rows(0), layer_rows(layers - 1)
    zero = jnp.zeros((segs, LANES), F32)
    here, below, total = lax.fori_loop(
        0, layers - 1, weigh, (resid_ref[first, :] + extra_ref[first, :], zero, zero), unroll=4
    )
    out = diag_ref[last, :] * here + below
    plane_ref[last, :] = out
    part_ref[...] = jnp.sum(total + here * out, axis=0, keepdims=True)


def gather_blocks(slots, plane_ref, cell_refs, outs):
    halves = halves_of(slots)
    wide = min(slots, LANES)

    for cells, out in zip(cell_refs, outs):

        def gather(line, carried, cells=cells, out=out):
            block, half = line // halves, line % halves
            for slot in range(0, wide, 16):
                rows = [plane_ref[pl.ds(cells[line, slot + step], 1), :] for step in range(16)]
                place = pl.ds(pl.multiple_of(half * wide + slot, 16), 16)
                out[block, place, :] = jnp.concatenate(rows, axis=0).astype(BF16)
            return carried

        lax.fori_loop(0, cells.shape[0], gather, 0)


def put_sum(slots, total, outs):
    high = total.astype(BF16).astype(F32)
    middle = (total - high).astype(BF16).astype(F32)
    low = total - high - middle
    row = lax.broadcasted_iota(I32, (TAIL, LANES), 0)
    tail = jnp.where(row == 0, high, jnp.where(row == 1, middle, jnp.where(row == 2, low, 0.0)))

    def one(ref, i, block, carried):
        ref[i, slots:] = tail.astype(BF16)
        return carried

    each(outs, None, one)


def pick_kernel(
    slots, chunks, plane_in, part_ref, lower_ref, upper_ref, off_ref, bottom_ref, prod_ref, *rest
):
    cell_refs = rest[:chunks]
    plane_ref, weighted_ref, sum_ref = rest[chunks : chunks + 3]
    outs, sem = rest[chunks + 3 : -1], rest[-1]
    segs = lower_ref.shape[0]
    first, last = pl.ds(0, segs), pl.ds(plane_ref.shape[0] - segs, segs)
    plane_ref[first, :] = plane_ref[first, :] + lower_ref[...]
    plane_ref[last, :] = plane_ref[last, :] + off_ref[...] * upper_ref[...]
    copy = pltpu.make_async_copy(plane_ref, weighted_ref, sem)
    copy.start()
    rims = bottom_ref[...] * lower_ref[...] + prod_ref[...] * upper_ref[...]
    total = jnp.sum(part_ref[...] + jnp.sum(rims, axis=0, keepdims=True), axis=1, keepdims=True)
    total = jnp.broadcast_to(total, (1, LANES))
    sum_ref[...] = total
    put_sum(slots, total, outs)
    gather_blocks(slots, plane_ref, cell_refs, outs)
    copy.wait()


def repick_kernel(slots, chunks, plane_ref, sum_ref, *rest):
    cell_refs, outs = rest[:chunks], rest[chunks:]
    put_sum(slots, sum_ref[...], outs)
    gather_blocks(slots, plane_ref, cell_refs, outs)


def unpacked(slots, firsts, pos, chunks, total):
    lane = lax.broadcasted_iota(I32, pos.shape, 1).astype(F32)
    wide = min(slots, LANES)

    def one(ref, i, block, total):
        for start in range(0, slots, wide):
            base = jnp.asarray(block * slots + start, I32).astype(F32)
            chosen = (pos - base == lane).astype(F32).astype(BF16)
            total = total + jnp.dot(
                chosen[:, :wide], ref[i, start : start + wide], preferred_element_type=F32
            )
        return total

    return each(chunks, firsts, one, total)


def unpack_kernel(slots, firsts, pos_ref, *rest):
    chunks, (places_ref, total_ref) = rest[:-2], rest[-2:]
    count = pos_ref.shape[1]
    pos = jnp.transpose(jnp.broadcast_to(pos_ref[...], (LANES, count)).astype(F32))
    places_ref[...] = pos
    total_ref[...] = unpacked(slots, firsts, pos, chunks, jnp.zeros((count, LANES), F32))


def last_unpack_kernel(slots, firsts, places_ref, total_ref, *rest):
    chunks, out_ref = rest[:-1], rest[-1]
    out_ref[...] = unpacked(slots, firsts, places_ref[...], chunks, total_ref[...]).astype(BF16)


def sum_kernel(slots, after_ref, *rest):
    chunks, out_ref = rest[:-1], rest[-1]

    def one(ref, i, block, total):
        tail = ref[i, slots:].astype(F32)
        return total + tail[0:1] + tail[1:2] + tail[2:3]

    out_ref[...] = each(chunks, None, one, jnp.zeros((1, LANES), F32))


def shape_of(shape, dtype):
    return jax.ShapeDtypeStruct(shape, dtype)


def params(mib):
    return pltpu.CompilerParams(vmem_limit_bytes=mib << 20)


def in_hbm(*arrays):
    return [pltpu.with_memory_space_constraint(array, pltpu.HBM) for array in arrays]


def call(kernel, args, in_specs, out_shape, out_specs, scratch=(), aliases=None, us=1.0):
    return pl.pallas_call(
        kernel,
        out_shape=tuple(out_shape),
        in_specs=list(in_specs),
        out_specs=tuple(out_specs),
        scratch_shapes=list(scratch),
        input_output_aliases=aliases or {},
        compiler_params=params(8),
        cost_estimate=pl.CostEstimate(
            flops=0, bytes_accessed=int(us * HBM_BYTES_PER_US), transcendentals=0
        ),
    )(*args)


def shards(tdi_data, noise_diag, noise_off, src_blocks, owner_dev, layer_in, seg_in):
    groups = lax.axis_size("band") * lax.axis_size("tm")
    _, layers, segs, bins = tdi_data.shape
    count = src_blocks.shape[0]
    slots = 2 * count // groups
    halves = halves_of(slots)
    cell_count = layers * segs
    direct = groups == 8
    if direct:
        sizes, first_out = [1] * groups, [7, 6, 5, 4, 3, 2, 1, 0]
        first_back, second_back = [7, 6, 5, 4, 3, 2, 1], [0]
        first_in, second_in = [0, 7, 6], [5, 4, 3, 2, 1]
        early, late = [0, 7, 6, 5], [4, 3, 2, 1]
    else:
        sizes, first_out = [groups], [0]
        first_back, second_back = [0], []
        first_in, second_in = [0], []
        early, late = [], [0]
    total = len(sizes)

    def exchanged(number, block):
        if not direct:
            return lax.all_to_all(block, AXES, split_axis=0, concat_axis=0, tiled=True)
        if number == 0:
            return block
        return lax.ppermute(block, AXES, [(i, i ^ number) for i in range(groups)])

    blocks = [shape_of((size, slots + TAIL, bins), BF16) for size in sizes]
    plane = pltpu.VMEM((cell_count, bins), F32)
    rim = shape_of((segs, bins), F32)
    line = shape_of((1, bins), F32)
    tdi = tdi_data.reshape(cell_count, bins)
    diag = noise_diag.reshape(cell_count, bins)
    off = noise_off.reshape(cell_count, bins)

    arrived = [None] * total
    pos, *packed = call(
        functools.partial(pack_kernel, slots, groups, direct, first_out),
        in_hbm(
            owner_dev.reshape(1, count),
            layer_in.reshape(1, count),
            seg_in.reshape(1, count),
            src_blocks.reshape(count, bins),
        ),
        [HBM] * 4,
        [pltpu.VMEM((1, count), I32)] + [blocks[k] for k in first_out],
        [VMEM] * (1 + len(first_out)),
        [pltpu.VMEM((1, count), I32)] * 3
        + [pltpu.VMEM((count, 2 * bins), BF16), pltpu.SemaphoreType.DMA((4,))],
        us=3.0,
    )
    for k, block in zip(first_out, packed):
        arrived[k] = exchanged(k, block)

    cells = [None] * total

    def scratch_of(step):
        size = sum(sizes[k] for k in step)
        return [
            pltpu.VMEM((size * slots, bins), F32),
            pltpu.SMEM((size * halves, LANES), I32),
            pltpu.SemaphoreType.DMA,
        ]

    def lines_of(step):
        return shape_of((sum(sizes[k] for k in step) * halves, LANES), I32)

    def split_lines(step, joined):
        start = 0
        for k in step:
            stop = start + sizes[k] * halves
            cells[k] = joined[start:stop]
            start = stop

    resid, extra, low, high, off_last, joined = call(
        functools.partial(first_scatter_kernel, slots, segs),
        in_hbm(tdi, off) + [arrived[k] for k in first_in],
        [HBM] * 2 + [VMEM] * len(first_in),
        [plane] * 2 + [rim] * 3 + [lines_of(first_in)],
        [VMEM] * 6,
        scratch_of(first_in) + [pltpu.SemaphoreType.DMA((2,))],
        us=3.0,
    )
    split_lines(first_in, joined)
    bottom, product = call(
        functools.partial(rim_kernel, slots, layers),
        [low, high, off_last, *arrived],
        [VMEM] * (3 + total),
        (rim, rim),
        (VMEM, VMEM),
        us=0.3,
    )
    lower_rim = passed_along(product, "band", 1)
    upper_rim = passed_along(bottom, "band", -1)
    step = second_in or [0]
    resid, extra, diag_in, off_in, joined = call(
        functools.partial(scatter_kernel, slots, segs),
        [resid, extra] + in_hbm(diag, off) + [arrived[k] for k in second_in],
        [VMEM] * 2 + [HBM] * 2 + [VMEM] * len(second_in),
        [plane] * 4 + [lines_of(step)],
        [VMEM] * 5,
        scratch_of(step) + [pltpu.SemaphoreType.DMA((2,))],
        {0: 0, 1: 1},
        us=3.5,
    )
    if second_in:
        split_lines(second_in, joined)
    weighed, part = call(
        functools.partial(weigh_kernel, segs, layers),
        (resid, extra, diag_in, off_in),
        [VMEM] * 4,
        (plane, line),
        (VMEM, VMEM),
        us=2.4,
    )
    returned = [None] * total
    weighed, weighted, summed, *picked = call(
        functools.partial(pick_kernel, slots, len(first_back)),
        (weighed, part, lower_rim, upper_rim, off_last, bottom, product)
        + tuple(cells[k] for k in first_back),
        [VMEM] * 7 + [SMEM] * len(first_back),
        [plane, shape_of((cell_count, bins), F32), line] + [blocks[k] for k in first_back],
        [VMEM, HBM, VMEM] + [VMEM] * len(first_back),
        [pltpu.SemaphoreType.DMA],
        {0: 0},
        us=2.5,
    )
    for k, block in zip(first_back, picked):
        returned[k] = exchanged(k, block)
    if second_back:
        picked = call(
            functools.partial(repick_kernel, slots, len(second_back)),
            (weighed, summed) + tuple(cells[k] for k in second_back),
            [VMEM] * 2 + [SMEM] * len(second_back),
            [blocks[k] for k in second_back],
            [VMEM] * len(second_back),
            us=0.5,
        )
        for k, block in zip(second_back, picked):
            returned[k] = exchanged(k, block)

    places, grads = call(
        functools.partial(unpack_kernel, slots, early),
        [pos] + [returned[k] for k in early],
        [VMEM] * (1 + len(early)),
        [pltpu.VMEM((count, LANES), F32)] * 2,
        (VMEM, VMEM),
    )
    (total_sum,) = call(
        functools.partial(sum_kernel, slots),
        [places] + returned,
        [VMEM] * (1 + total),
        (line,),
        (VMEM,),
        us=0.1,
    )
    chan = lax.axis_size("chan")
    other_sum = lax.ppermute(total_sum, "chan", [(i, i ^ 1) for i in range(chan)])
    cells_all = chan * groups * cell_count * bins
    log_like = (total_sum + other_sum)[0, :1] * (-0.5 / cells_all)
    (grads,) = call(
        functools.partial(last_unpack_kernel, slots, late),
        [places, grads] + [returned[k] for k in late],
        [VMEM] * (2 + len(late)),
        (shape_of((count, bins), BF16),),
        (VMEM,),
    )
    return (
        weighted.reshape(tdi_data.shape),
        log_like,
        grads.reshape(src_blocks.shape),
    )


def solution(mesh):
    planes = P(("grp", "chan"), "band", "tm", None)
    lists = P(("grp", "band", "tm"))
    return jax.shard_map(
        shards,
        mesh=mesh,
        in_specs=(
            planes,
            planes,
            planes,
            P(("grp", "band", "tm"), "chan", None),
            P(("grp", "band", "tm"), None),
            lists,
            lists,
        ),
        out_specs=(planes, P("grp"), P(("grp", "band", "tm"), "chan", None)),
        check_vma=False,
    )
```

```python
import functools

import jax
import jax.numpy as jnp
from jax import lax
from jax.experimental import pallas as pl
from jax.experimental.pallas import tpu as pltpu
from jax.sharding import PartitionSpec as P

LANES = 128
TAIL = 16
AXES = ("band", "tm")
VMEM = pl.BlockSpec(memory_space=pltpu.VMEM)
SMEM = pl.BlockSpec(memory_space=pltpu.SMEM)
HBM = pl.BlockSpec(memory_space=pltpu.HBM)
HBM_BYTES_PER_US = 3_300_000
F32 = jnp.float32
BF16 = jnp.bfloat16
I32 = jnp.int32


def passed_along(value, axis, steps):
    count = lax.axis_size(axis)
    leading, last = (max(0, -steps), min(count, count - steps))
    return lax.ppermute(value, axis, [(source, source + steps) for source in range(leading, last)])


def halves_of(slots):
    return max(1, slots // LANES)


def few(count):
    return count <= 8


def each(refs, firsts, body, carried=0):
    if firsts is None:
        firsts = [sum(ref.shape[0] for ref in refs[:i]) for i in range(len(refs))]
    for ref, first in zip(refs, firsts):
        length = ref.shape[0]
        carried = lax.fori_loop(
            0,
            length,
            lambda i, value, ref=ref, first=first: body(ref, i, first + i, value),
            carried,
            unroll=few(length),
        )
    return carried


def pack_kernel(
    slots, groups, direct, firsts, own_hbm, layer_hbm, seg_hbm, src_hbm, tdi_hbm,
    resid_ref, pos_ref, *rest
):
    outs, (own_ref, layer_ref, seg_ref, wide_ref, sems) = rest[:-5], rest[-5:]
    src_ref = wide_ref.at[:, pl.ds(0, LANES)]
    copies = [
        pltpu.make_async_copy(source, target, sems.at[i])
        for i, (source, target) in enumerate(
            (
                (own_hbm, own_ref),
                (layer_hbm, layer_ref),
                (seg_hbm, seg_ref),
                (src_hbm, src_ref),
                (tdi_hbm, resid_ref),
            )
        )
    ]
    for copy in copies:
        copy.start()
    count = own_ref.shape[1]
    width = min(count, 256)
    before = (
        lax.broadcasted_iota(I32, (width, width), 0) < lax.broadcasted_iota(I32, (width, width), 1)
    ).astype(F32).astype(BF16)
    copies[0].wait()
    own = own_ref[...]
    if direct:
        own = own ^ (lax.axis_index("band") * lax.axis_size("tm") + lax.axis_index("tm"))
    rows = max(16, groups)
    owned = (lax.broadcasted_iota(I32, (rows, count), 0) == own).astype(F32)
    carry = jnp.zeros((rows, 1), F32)
    ranks = []
    for start in range(0, count, width):
        part = owned[:, start : start + width]
        earlier = jnp.dot(part.astype(BF16), before, preferred_element_type=F32) + carry
        ranks.append(jnp.sum(part * earlier, axis=0, keepdims=True))
        carry = carry + jnp.sum(part, axis=1, keepdims=True)
    pos = own * slots + jnp.concatenate(ranks, axis=1).astype(I32)
    pos_ref[...] = pos
    copies[1].wait()
    copies[2].wait()
    even = lax.broadcasted_iota(I32, (LANES, count), 0) % 2 == 0
    names = jnp.where(even, layer_ref[...], seg_ref[...]).astype(F32)
    wide_ref[:, LANES:] = jnp.transpose(names).astype(BF16)
    copies[3].wait()
    tall = max(slots, LANES)
    slot = lax.broadcasted_iota(I32, (tall, count), 0)
    lane_pair = lax.broadcasted_iota(I32, (tall, LANES), 1) // 2
    tail_row = lax.broadcasted_iota(I32, (TAIL, LANES), 0)

    def tail_of(named, row):
        tail = jnp.zeros((TAIL, LANES), F32)
        for half in range(halves_of(slots)):
            pair = named[row : row + 2, half * LANES : (half + 1) * LANES]
            for i in range(2):
                tail = jnp.where(tail_row == 2 * half + i, pair[i : i + 1], tail)
        return tail.astype(BF16)

    def one(ref, i, block, named):
        chosen = (slot == pos - block * slots).astype(F32).astype(BF16)
        if slots < LANES:
            chosen = jnp.where(slot < slots, chosen, jnp.zeros_like(chosen))
        found = jnp.dot(chosen, wide_ref[...], preferred_element_type=F32)
        ref[i, :slots] = found[:slots, :LANES].astype(BF16)
        if few(groups):
            return jnp.where(lane_pair == block, found[:, LANES:], named)
        ref[i, slots:] = tail_of(jnp.transpose(found[:, LANES:]), 0)
        return named

    named = each(outs, firsts, one, jnp.zeros((tall, LANES), F32))
    if few(groups):
        named = jnp.transpose(named)
        for ref, first in zip(outs, firsts):
            for i in range(ref.shape[0]):
                ref[i, slots:] = tail_of(named, 2 * (first + i))
    copies[4].wait()


def cells_of(ref, i, slots, segs):
    tail = ref[i, slots:].astype(F32)
    return [
        tail[2 * half : 2 * half + 1] * segs + tail[2 * half + 1 : 2 * half + 2]
        for half in range(halves_of(slots))
    ]


def rim_kernel(slots, layers, after_ref, low_ref, high_ref, off_ref, *rest):
    chunks, (bottom_ref, prod_ref) = rest[:-2], rest[-2:]
    segs = low_ref.shape[0]
    line = lax.broadcasted_iota(I32, (2 * segs, LANES), 0)
    wanted = jnp.where(line < segs, line, line + (layers - 2) * segs).astype(F32)
    wide = min(slots, LANES)

    def one(ref, i, block, total):
        for half, cells in enumerate(cells_of(ref, i, slots, segs)):
            chosen = (wanted == cells).astype(F32).astype(BF16)
            total = total + jnp.dot(
                chosen[:, :wide],
                ref[i, half * wide : (half + 1) * wide],
                preferred_element_type=F32,
            )
        return total

    model = each(chunks, None, one, jnp.zeros((2 * segs, LANES), F32))
    bottom_ref[...] = low_ref[...] - model[:segs]
    prod_ref[...] = off_ref[...] * (high_ref[...] - model[segs:])


def scatter_blocks(slots, segs, chunks, resid_ref, extra_ref, cell_ref, blocks, cells, sem, ready):
    halves = halves_of(slots)
    wide = min(slots, LANES)

    def name(ref, i, block, carried):
        for half, row in enumerate(cells_of(ref, i, slots, segs)):
            cell_ref[pl.ds(block * halves + half, 1), :] = row.astype(I32)
        return carried

    each(chunks, None, name)
    copy = pltpu.make_async_copy(cell_ref, cells, sem)
    copy.start()

    def widen(ref, i, block, carried):
        blocks[pl.ds(pl.multiple_of(block * slots, slots), slots), :] = ref[i, :slots].astype(F32)
        return carried

    each(chunks, None, widen)
    ready()
    copy.wait()

    def scatter(line, carried):
        for slot in range(0, wide, 4):
            turns = []
            for step, plane in enumerate((resid_ref, extra_ref)):
                one, two = cells[line, slot + step], cells[line, slot + step + 2]
                first = blocks[pl.ds(line * wide + slot + step, 1), :]
                second = blocks[pl.ds(line * wide + slot + step + 2, 1), :]
                second = second + jnp.where(one == two, first, 0.0)
                one, two = pl.ds(one, 1), pl.ds(two, 1)
                turns.append((plane, one, two, plane[one, :] - first, plane[two, :] - second))
            for plane, one, two, first, second in turns:
                plane[one, :] = first
                plane[two, :] = second
        return carried

    lax.fori_loop(0, cell_ref.shape[0], scatter, 0)


def first_scatter_kernel(slots, segs, resid_in, diag_hbm, off_hbm, *rest):
    chunks, outs, (blocks, cells, sem, sems) = rest[:-11], rest[-11:-4], rest[-4:]
    resid_ref, extra_ref, diag_ref, low_ref, high_ref, last_ref, cell_ref = outs
    size = resid_ref.shape[0]
    copies = [
        pltpu.make_async_copy(off_hbm.at[pl.ds(size - segs, segs)], last_ref, sems.at[0]),
        pltpu.make_async_copy(diag_hbm, diag_ref, sems.at[1]),
    ]
    for copy in copies:
        copy.start()

    def ready():
        extra_ref[...] = jnp.zeros_like(extra_ref)
        low_ref[...] = resid_ref[:segs]
        high_ref[...] = resid_ref[size - segs :]

    scatter_blocks(slots, segs, chunks, resid_ref, extra_ref, cell_ref, blocks, cells, sem, ready)
    for copy in copies:
        copy.wait()


def scatter_kernel(slots, segs, resid_in, extra_in, *rest):
    chunks, (resid_ref, extra_ref, cell_ref, blocks, cells, sem) = rest[:-6], rest[-6:]
    scatter_blocks(
        slots, segs, chunks, resid_ref, extra_ref, cell_ref, blocks, cells, sem, lambda: None
    )


def last_scatter_kernel(slots, segs, resid_in, extra_in, off_hbm, *rest):
    chunks, outs, (blocks, cells, sem, off_sem) = rest[:-8], rest[-8:-4], rest[-4:]
    resid_ref, extra_ref, off_ref, cell_ref = outs
    copy = pltpu.make_async_copy(off_hbm, off_ref, off_sem)
    copy.start()
    if chunks:
        scatter_blocks(
            slots, segs, chunks, resid_ref, extra_ref, cell_ref, blocks, cells, sem, lambda: None
        )
    copy.wait()


def weigh_kernel(segs, layers, resid_ref, extra_ref, diag_ref, off_ref, plane_ref, part_ref):
    def layer_rows(layer):
        return pl.ds(pl.multiple_of(layer * segs, segs), segs)

    def weigh(layer, carried):
        here, below, total = carried
        place, above_place = layer_rows(layer), layer_rows(layer + 1)
        above = resid_ref[above_place, :] + extra_ref[above_place, :]
        coupling = off_ref[place, :]
        out = diag_ref[place, :] * here + coupling * above + below
        plane_ref[place, :] = out
        return above, coupling * here, total + here * out

    first, last = layer_rows(0), layer_rows(layers - 1)
    zero = jnp.zeros((segs, LANES), F32)
    here, below, total = lax.fori_loop(
        0, layers - 1, weigh, (resid_ref[first, :] + extra_ref[first, :], zero, zero), unroll=4
    )
    out = diag_ref[last, :] * here + below
    plane_ref[last, :] = out
    part_ref[...] = jnp.sum(total + here * out, axis=0, keepdims=True)


def gather_blocks(slots, plane_ref, cell_refs, outs):
    halves = halves_of(slots)
    wide = min(slots, LANES)

    for cells, out in zip(cell_refs, outs):

        def gather(line, carried, cells=cells, out=out):
            block, half = line // halves, line % halves
            for slot in range(0, wide, 16):
                rows = [plane_ref[pl.ds(cells[line, slot + step], 1), :] for step in range(16)]
                place = pl.ds(pl.multiple_of(half * wide + slot, 16), 16)
                out[block, place, :] = jnp.concatenate(rows, axis=0).astype(BF16)
            return carried

        lax.fori_loop(0, cells.shape[0], gather, 0)


def put_sum(slots, total, outs):
    high = total.astype(BF16).astype(F32)
    middle = (total - high).astype(BF16).astype(F32)
    low = total - high - middle
    row = lax.broadcasted_iota(I32, (TAIL, LANES), 0)
    tail = jnp.where(row == 0, high, jnp.where(row == 1, middle, jnp.where(row == 2, low, 0.0)))

    def one(ref, i, block, carried):
        ref[i, slots:] = tail.astype(BF16)
        return carried

    each(outs, None, one)


def pick_kernel(
    slots, chunks, plane_in, part_ref, lower_ref, upper_ref, off_ref, bottom_ref, prod_ref, *rest
):
    cell_refs = rest[:chunks]
    plane_ref, weighted_ref, sum_ref = rest[chunks : chunks + 3]
    outs, sem = rest[chunks + 3 : -1], rest[-1]
    segs = lower_ref.shape[0]
    first, last = pl.ds(0, segs), pl.ds(plane_ref.shape[0] - segs, segs)
    plane_ref[first, :] = plane_ref[first, :] + lower_ref[...]
    plane_ref[last, :] = plane_ref[last, :] + off_ref[...] * upper_ref[...]
    copy = pltpu.make_async_copy(plane_ref, weighted_ref, sem)
    copy.start()
    rims = bottom_ref[...] * lower_ref[...] + prod_ref[...] * upper_ref[...]
    total = jnp.sum(part_ref[...] + jnp.sum(rims, axis=0, keepdims=True), axis=1, keepdims=True)
    total = jnp.broadcast_to(total, (1, LANES))
    sum_ref[...] = total
    put_sum(slots, total, outs)
    gather_blocks(slots, plane_ref, cell_refs, outs)
    copy.wait()


def repick_kernel(slots, chunks, plane_ref, sum_ref, *rest):
    cell_refs, outs = rest[:chunks], rest[chunks:]
    put_sum(slots, sum_ref[...], outs)
    gather_blocks(slots, plane_ref, cell_refs, outs)


def unpacked(slots, firsts, pos, chunks, total):
    lane = lax.broadcasted_iota(I32, pos.shape, 1).astype(F32)
    wide = min(slots, LANES)

    def one(ref, i, block, total):
        for start in range(0, slots, wide):
            base = jnp.asarray(block * slots + start, I32).astype(F32)
            chosen = (pos - base == lane).astype(F32).astype(BF16)
            total = total + jnp.dot(
                chosen[:, :wide], ref[i, start : start + wide], preferred_element_type=F32
            )
        return total

    return each(chunks, firsts, one, total)


def unpack_kernel(slots, firsts, pos_ref, *rest):
    chunks, (places_ref, total_ref) = rest[:-2], rest[-2:]
    count = pos_ref.shape[1]
    pos = jnp.transpose(jnp.broadcast_to(pos_ref[...], (LANES, count)).astype(F32))
    places_ref[...] = pos
    total_ref[...] = unpacked(slots, firsts, pos, chunks, jnp.zeros((count, LANES), F32))


def last_unpack_kernel(slots, firsts, places_ref, total_ref, *rest):
    chunks, out_ref = rest[:-1], rest[-1]
    out_ref[...] = unpacked(slots, firsts, places_ref[...], chunks, total_ref[...]).astype(BF16)


def sum_kernel(slots, after_ref, *rest):
    chunks, out_ref = rest[:-1], rest[-1]

    def one(ref, i, block, total):
        tail = ref[i, slots:].astype(F32)
        return total + tail[0:1] + tail[1:2] + tail[2:3]

    out_ref[...] = each(chunks, None, one, jnp.zeros((1, LANES), F32))


def shape_of(shape, dtype):
    return jax.ShapeDtypeStruct(shape, dtype)


def params(mib):
    return pltpu.CompilerParams(vmem_limit_bytes=mib << 20)


def in_hbm(*arrays):
    return [pltpu.with_memory_space_constraint(array, pltpu.HBM) for array in arrays]


def call(kernel, args, in_specs, out_shape, out_specs, scratch=(), aliases=None, us=1.0):
    return pl.pallas_call(
        kernel,
        out_shape=tuple(out_shape),
        in_specs=list(in_specs),
        out_specs=tuple(out_specs),
        scratch_shapes=list(scratch),
        input_output_aliases=aliases or {},
        compiler_params=params(8),
        cost_estimate=pl.CostEstimate(
            flops=0, bytes_accessed=int(us * HBM_BYTES_PER_US), transcendentals=0
        ),
    )(*args)


def shards(tdi_data, noise_diag, noise_off, src_blocks, owner_dev, layer_in, seg_in):
    groups = lax.axis_size("band") * lax.axis_size("tm")
    _, layers, segs, bins = tdi_data.shape
    count = src_blocks.shape[0]
    slots = 2 * count // groups
    halves = halves_of(slots)
    cell_count = layers * segs
    direct = groups == 8
    if direct:
        order = [7, 6, 5, 4, 3, 2, 1]
        sizes, first_out = [1] * groups, order + [0]
        first_back, second_back = order, [0]
        first_in, second_in, last_in = [0] + order[:2], order[2:3], order[3:]
        early, late = [0] + order[:3], order[3:]
    else:
        sizes, first_out = [groups], [0]
        first_back, second_back = [0], []
        first_in, second_in, last_in = [0], [], []
        early, late = [], [0]
    total = len(sizes)

    def exchanged(number, block):
        if not direct:
            return lax.all_to_all(block, AXES, split_axis=0, concat_axis=0, tiled=True)
        if number == 0:
            return block
        return lax.ppermute(block, AXES, [(i, i ^ number) for i in range(groups)])

    blocks = [shape_of((size, slots + TAIL, bins), BF16) for size in sizes]
    plane = pltpu.VMEM((cell_count, bins), F32)
    rim = shape_of((segs, bins), F32)
    line = shape_of((1, bins), F32)
    tdi = tdi_data.reshape(cell_count, bins)
    diag = noise_diag.reshape(cell_count, bins)
    off = noise_off.reshape(cell_count, bins)

    arrived = [None] * total
    resid, pos, *packed = call(
        functools.partial(pack_kernel, slots, groups, direct, first_out),
        in_hbm(
            owner_dev.reshape(1, count),
            layer_in.reshape(1, count),
            seg_in.reshape(1, count),
            src_blocks.reshape(count, bins),
            tdi,
        ),
        [HBM] * 5,
        [plane, pltpu.VMEM((1, count), I32)] + [blocks[k] for k in first_out],
        [VMEM] * (2 + len(first_out)),
        [pltpu.VMEM((1, count), I32)] * 3
        + [pltpu.VMEM((count, 2 * bins), BF16), pltpu.SemaphoreType.DMA((5,))],
        us=3.0,
    )
    for k, block in zip(first_out, packed):
        arrived[k] = exchanged(k, block)

    cells = [None] * total

    def scratch_of(step):
        size = sum(sizes[k] for k in step)
        return [
            pltpu.VMEM((size * slots, bins), F32),
            pltpu.SMEM((size * halves, LANES), I32),
            pltpu.SemaphoreType.DMA,
        ]

    def lines_of(step):
        return shape_of((sum(sizes[k] for k in step) * halves, LANES), I32)

    def split_lines(step, joined):
        start = 0
        for k in step:
            stop = start + sizes[k] * halves
            cells[k] = joined[start:stop]
            start = stop

    resid, extra, diag_in, low, high, off_last, joined = call(
        functools.partial(first_scatter_kernel, slots, segs),
        [resid] + in_hbm(diag, off) + [arrived[k] for k in first_in],
        [VMEM] + [HBM] * 2 + [VMEM] * len(first_in),
        [plane] * 3 + [rim] * 3 + [lines_of(first_in)],
        [VMEM] * 7,
        scratch_of(first_in) + [pltpu.SemaphoreType.DMA((2,))],
        {0: 0},
        us=2.5,
    )
    split_lines(first_in, joined)
    if second_in:
        resid, extra, joined = call(
            functools.partial(scatter_kernel, slots, segs),
            [resid, extra] + [arrived[k] for k in second_in],
            [VMEM] * (2 + len(second_in)),
            [plane] * 2 + [lines_of(second_in)],
            [VMEM] * 3,
            scratch_of(second_in),
            {0: 0, 1: 1},
            us=0.9,
        )
        split_lines(second_in, joined)
    bottom, product = call(
        functools.partial(rim_kernel, slots, layers),
        [joined, low, high, off_last, *arrived],
        [VMEM] * (4 + total),
        (rim, rim),
        (VMEM, VMEM),
        us=0.3,
    )
    lower_rim = passed_along(product, "band", 1)
    upper_rim = passed_along(bottom, "band", -1)
    step = last_in or [0]
    resid, extra, off_in, joined = call(
        functools.partial(last_scatter_kernel, slots, segs),
        [resid, extra] + in_hbm(off) + [arrived[k] for k in last_in],
        [VMEM] * 2 + [HBM] + [VMEM] * len(last_in),
        [plane] * 3 + [lines_of(step)],
        [VMEM] * 4,
        scratch_of(step) + [pltpu.SemaphoreType.DMA],
        {0: 0, 1: 1},
        us=2.5,
    )
    if last_in:
        split_lines(last_in, joined)
    weighed, part = call(
        functools.partial(weigh_kernel, segs, layers),
        (resid, extra, diag_in, off_in),
        [VMEM] * 4,
        (plane, line),
        (VMEM, VMEM),
        us=2.4,
    )
    returned = [None] * total
    weighed, weighted, summed, *picked = call(
        functools.partial(pick_kernel, slots, len(first_back)),
        (weighed, part, lower_rim, upper_rim, off_last, bottom, product)
        + tuple(cells[k] for k in first_back),
        [VMEM] * 7 + [SMEM] * len(first_back),
        [plane, shape_of((cell_count, bins), F32), line] + [blocks[k] for k in first_back],
        [VMEM, HBM, VMEM] + [VMEM] * len(first_back),
        [pltpu.SemaphoreType.DMA],
        {0: 0},
        us=2.5,
    )
    for k, block in zip(first_back, picked):
        returned[k] = exchanged(k, block)
    if second_back:
        picked = call(
            functools.partial(repick_kernel, slots, len(second_back)),
            (weighed, summed) + tuple(cells[k] for k in second_back),
            [VMEM] * 2 + [SMEM] * len(second_back),
            [blocks[k] for k in second_back],
            [VMEM] * len(second_back),
            us=0.5,
        )
        for k, block in zip(second_back, picked):
            returned[k] = exchanged(k, block)

    places, grads = call(
        functools.partial(unpack_kernel, slots, early),
        [pos] + [returned[k] for k in early],
        [VMEM] * (1 + len(early)),
        [pltpu.VMEM((count, LANES), F32)] * 2,
        (VMEM, VMEM),
    )
    (total_sum,) = call(
        functools.partial(sum_kernel, slots),
        [places] + returned,
        [VMEM] * (1 + total),
        (line,),
        (VMEM,),
        us=0.1,
    )
    chan = lax.axis_size("chan")
    other_sum = lax.ppermute(total_sum, "chan", [(i, i ^ 1) for i in range(chan)])
    cells_all = chan * groups * cell_count * bins
    log_like = (total_sum + other_sum)[0, :1] * (-0.5 / cells_all)
    (grads,) = call(
        functools.partial(last_unpack_kernel, slots, late),
        [places, grads] + [returned[k] for k in late],
        [VMEM] * (2 + len(late)),
        (shape_of((count, bins), BF16),),
        (VMEM,),
    )
    return (
        weighted.reshape(tdi_data.shape),
        log_like,
        grads.reshape(src_blocks.shape),
    )


def solution(mesh):
    planes = P(("grp", "chan"), "band", "tm", None)
    lists = P(("grp", "band", "tm"))
    return jax.shard_map(
        shards,
        mesh=mesh,
        in_specs=(
            planes,
            planes,
            planes,
            P(("grp", "band", "tm"), "chan", None),
            P(("grp", "band", "tm"), None),
            lists,
            lists,
        ),
        out_specs=(planes, P("grp"), P(("grp", "band", "tm"), "chan", None)),
        check_vma=False,
    )
```

```python
import functools

import jax
import jax.numpy as jnp
from jax import lax
from jax.experimental import pallas as pl
from jax.experimental.pallas import tpu as pltpu
from jax.sharding import PartitionSpec as P

LANES = 128
TAIL = 16
AXES = ("band", "tm")
VMEM = pl.BlockSpec(memory_space=pltpu.VMEM)
SMEM = pl.BlockSpec(memory_space=pltpu.SMEM)
HBM = pl.BlockSpec(memory_space=pltpu.HBM)
HBM_BYTES_PER_US = 3_300_000
F32 = jnp.float32
BF16 = jnp.bfloat16
I32 = jnp.int32


def passed_along(value, axis, steps):
    count = lax.axis_size(axis)
    leading, last = (max(0, -steps), min(count, count - steps))
    return lax.ppermute(value, axis, [(source, source + steps) for source in range(leading, last)])


def halves_of(slots):
    return max(1, slots // LANES)


def few(count):
    return count <= 8


def each(refs, firsts, body, carried=0):
    if firsts is None:
        firsts = [sum(ref.shape[0] for ref in refs[:i]) for i in range(len(refs))]
    for ref, first in zip(refs, firsts):
        length = ref.shape[0]
        carried = lax.fori_loop(
            0,
            length,
            lambda i, value, ref=ref, first=first: body(ref, i, first + i, value),
            carried,
            unroll=few(length),
        )
    return carried


def pack_kernel(
    slots, groups, direct, firsts, own_hbm, layer_hbm, seg_hbm, src_hbm, tdi_hbm,
    resid_ref, pos_ref, *rest
):
    outs, (own_ref, layer_ref, seg_ref, wide_ref, sems) = rest[:-5], rest[-5:]
    src_ref = wide_ref.at[:, pl.ds(0, LANES)]
    copies = [
        pltpu.make_async_copy(source, target, sems.at[i])
        for i, (source, target) in enumerate(
            (
                (own_hbm, own_ref),
                (layer_hbm, layer_ref),
                (seg_hbm, seg_ref),
                (src_hbm, src_ref),
                (tdi_hbm, resid_ref),
            )
        )
    ]
    for copy in copies:
        copy.start()
    count = own_ref.shape[1]
    width = min(count, 256)
    before = (
        lax.broadcasted_iota(I32, (width, width), 0) < lax.broadcasted_iota(I32, (width, width), 1)
    ).astype(F32).astype(BF16)
    copies[0].wait()
    own = own_ref[...]
    if direct:
        own = own ^ (lax.axis_index("band") * lax.axis_size("tm") + lax.axis_index("tm"))
    rows = max(16, groups)
    owned = (lax.broadcasted_iota(I32, (rows, count), 0) == own).astype(F32)
    carry = jnp.zeros((rows, 1), F32)
    ranks = []
    for start in range(0, count, width):
        part = owned[:, start : start + width]
        earlier = jnp.dot(part.astype(BF16), before, preferred_element_type=F32) + carry
        ranks.append(jnp.sum(part * earlier, axis=0, keepdims=True))
        carry = carry + jnp.sum(part, axis=1, keepdims=True)
    pos = own * slots + jnp.concatenate(ranks, axis=1).astype(I32)
    pos_ref[...] = pos
    copies[1].wait()
    copies[2].wait()
    even = lax.broadcasted_iota(I32, (LANES, count), 0) % 2 == 0
    names = jnp.where(even, layer_ref[...], seg_ref[...]).astype(F32)
    wide_ref[:, LANES:] = jnp.transpose(names).astype(BF16)
    copies[3].wait()
    tall = max(slots, LANES)
    slot = lax.broadcasted_iota(I32, (tall, count), 0)
    lane_pair = lax.broadcasted_iota(I32, (tall, LANES), 1) // 2
    tail_row = lax.broadcasted_iota(I32, (TAIL, LANES), 0)

    def tail_of(named, row):
        tail = jnp.zeros((TAIL, LANES), F32)
        for half in range(halves_of(slots)):
            pair = named[row : row + 2, half * LANES : (half + 1) * LANES]
            for i in range(2):
                tail = jnp.where(tail_row == 2 * half + i, pair[i : i + 1], tail)
        return tail.astype(BF16)

    def one(ref, i, block, named):
        chosen = (slot == pos - block * slots).astype(F32).astype(BF16)
        if slots < LANES:
            chosen = jnp.where(slot < slots, chosen, jnp.zeros_like(chosen))
        found = jnp.dot(chosen, wide_ref[...], preferred_element_type=F32)
        ref[i, :slots] = found[:slots, :LANES].astype(BF16)
        if few(groups):
            return jnp.where(lane_pair == block, found[:, LANES:], named)
        ref[i, slots:] = tail_of(jnp.transpose(found[:, LANES:]), 0)
        return named

    named = each(outs, firsts, one, jnp.zeros((tall, LANES), F32))
    if few(groups):
        named = jnp.transpose(named)
        for ref, first in zip(outs, firsts):
            for i in range(ref.shape[0]):
                ref[i, slots:] = tail_of(named, 2 * (first + i))
    copies[4].wait()


def cells_of(ref, i, slots, segs):
    tail = ref[i, slots:].astype(F32)
    return [
        tail[2 * half : 2 * half + 1] * segs + tail[2 * half + 1 : 2 * half + 2]
        for half in range(halves_of(slots))
    ]


def rim_kernel(slots, layers, after_ref, low_ref, high_ref, off_ref, *rest):
    chunks, (bottom_ref, prod_ref) = rest[:-2], rest[-2:]
    segs = low_ref.shape[0]
    line = lax.broadcasted_iota(I32, (2 * segs, LANES), 0)
    wanted = jnp.where(line < segs, line, line + (layers - 2) * segs).astype(F32)
    wide = min(slots, LANES)

    def one(ref, i, block, total):
        for half, cells in enumerate(cells_of(ref, i, slots, segs)):
            chosen = (wanted == cells).astype(F32).astype(BF16)
            total = total + jnp.dot(
                chosen[:, :wide],
                ref[i, half * wide : (half + 1) * wide],
                preferred_element_type=F32,
            )
        return total

    model = each(chunks, None, one, jnp.zeros((2 * segs, LANES), F32))
    bottom_ref[...] = low_ref[...] - model[:segs]
    prod_ref[...] = off_ref[...] * (high_ref[...] - model[segs:])


def scatter_blocks(slots, segs, chunks, resid_ref, extra_ref, cell_ref, blocks, cells, sem, ready):
    halves = halves_of(slots)
    wide = min(slots, LANES)

    def name(ref, i, block, carried):
        for half, row in enumerate(cells_of(ref, i, slots, segs)):
            cell_ref[pl.ds(block * halves + half, 1), :] = row.astype(I32)
        return carried

    each(chunks, None, name)
    copy = pltpu.make_async_copy(cell_ref, cells, sem)
    copy.start()

    def widen(ref, i, block, carried):
        blocks[pl.ds(pl.multiple_of(block * slots, slots), slots), :] = ref[i, :slots].astype(F32)
        return carried

    each(chunks, None, widen)
    ready()
    copy.wait()

    def scatter(line, carried):
        for slot in range(0, wide, 4):
            turns = []
            for step, plane in enumerate((resid_ref, extra_ref)):
                one, two = cells[line, slot + step], cells[line, slot + step + 2]
                first = blocks[pl.ds(line * wide + slot + step, 1), :]
                second = blocks[pl.ds(line * wide + slot + step + 2, 1), :]
                second = second + jnp.where(one == two, first, 0.0)
                one, two = pl.ds(one, 1), pl.ds(two, 1)
                turns.append((plane, one, two, plane[one, :] - first, plane[two, :] - second))
            for plane, one, two, first, second in turns:
                plane[one, :] = first
                plane[two, :] = second
        return carried

    lax.fori_loop(0, cell_ref.shape[0], scatter, 0)


def first_scatter_kernel(slots, segs, resid_in, diag_hbm, off_hbm, *rest):
    chunks, outs, (blocks, cells, sem, sems) = rest[:-11], rest[-11:-4], rest[-4:]
    resid_ref, extra_ref, diag_ref, low_ref, high_ref, last_ref, cell_ref = outs
    size = resid_ref.shape[0]
    copies = [
        pltpu.make_async_copy(off_hbm.at[pl.ds(size - segs, segs)], last_ref, sems.at[0]),
        pltpu.make_async_copy(diag_hbm, diag_ref, sems.at[1]),
    ]
    for copy in copies:
        copy.start()

    def ready():
        extra_ref[...] = jnp.zeros_like(extra_ref)
        low_ref[...] = resid_ref[:segs]
        high_ref[...] = resid_ref[size - segs :]

    scatter_blocks(slots, segs, chunks, resid_ref, extra_ref, cell_ref, blocks, cells, sem, ready)
    for copy in copies:
        copy.wait()


def scatter_kernel(slots, segs, resid_in, extra_in, *rest):
    chunks, (resid_ref, extra_ref, cell_ref, blocks, cells, sem) = rest[:-6], rest[-6:]
    scatter_blocks(
        slots, segs, chunks, resid_ref, extra_ref, cell_ref, blocks, cells, sem, lambda: None
    )


def last_scatter_kernel(slots, segs, resid_in, extra_in, off_hbm, *rest):
    chunks, outs, (blocks, cells, sem, off_sem) = rest[:-8], rest[-8:-4], rest[-4:]
    resid_ref, extra_ref, off_ref, cell_ref = outs
    copy = pltpu.make_async_copy(off_hbm, off_ref, off_sem)
    copy.start()
    if chunks:
        scatter_blocks(
            slots, segs, chunks, resid_ref, extra_ref, cell_ref, blocks, cells, sem, lambda: None
        )
    copy.wait()


def weigh_kernel(segs, layers, resid_ref, extra_ref, diag_ref, off_ref, plane_ref, part_ref):
    def layer_rows(layer):
        return pl.ds(pl.multiple_of(layer * segs, segs), segs)

    def weigh(layer, carried):
        here, below, total = carried
        place, above_place = layer_rows(layer), layer_rows(layer + 1)
        above = resid_ref[above_place, :] + extra_ref[above_place, :]
        coupling = off_ref[place, :]
        out = diag_ref[place, :] * here + coupling * above + below
        plane_ref[place, :] = out
        return above, coupling * here, total + here * out

    first, last = layer_rows(0), layer_rows(layers - 1)
    zero = jnp.zeros((segs, LANES), F32)
    here, below, total = lax.fori_loop(
        0, layers - 1, weigh, (resid_ref[first, :] + extra_ref[first, :], zero, zero), unroll=4
    )
    out = diag_ref[last, :] * here + below
    plane_ref[last, :] = out
    part_ref[...] = jnp.sum(total + here * out, axis=0, keepdims=True)


def gather_blocks(slots, plane_ref, cell_refs, outs):
    halves = halves_of(slots)
    wide = min(slots, LANES)

    for cells, out in zip(cell_refs, outs):

        def gather(line, carried, cells=cells, out=out):
            block, half = line // halves, line % halves
            for slot in range(0, wide, 16):
                rows = [plane_ref[pl.ds(cells[line, slot + step], 1), :] for step in range(16)]
                place = pl.ds(pl.multiple_of(half * wide + slot, 16), 16)
                out[block, place, :] = jnp.concatenate(rows, axis=0).astype(BF16)
            return carried

        lax.fori_loop(0, cells.shape[0], gather, 0)


def put_sum(slots, total, outs):
    high = total.astype(BF16).astype(F32)
    middle = (total - high).astype(BF16).astype(F32)
    low = total - high - middle
    row = lax.broadcasted_iota(I32, (TAIL, LANES), 0)
    tail = jnp.where(row == 0, high, jnp.where(row == 1, middle, jnp.where(row == 2, low, 0.0)))

    def one(ref, i, block, carried):
        ref[i, slots:] = tail.astype(BF16)
        return carried

    each(outs, None, one)


def pick_kernel(
    slots, chunks, plane_in, part_ref, lower_ref, upper_ref, off_ref, bottom_ref, prod_ref, *rest
):
    cell_refs = rest[:chunks]
    plane_ref, weighted_ref, sum_ref = rest[chunks : chunks + 3]
    outs, sem = rest[chunks + 3 : -1], rest[-1]
    segs = lower_ref.shape[0]
    first, last = pl.ds(0, segs), pl.ds(plane_ref.shape[0] - segs, segs)
    plane_ref[first, :] = plane_ref[first, :] + lower_ref[...]
    plane_ref[last, :] = plane_ref[last, :] + off_ref[...] * upper_ref[...]
    copy = pltpu.make_async_copy(plane_ref, weighted_ref, sem)
    copy.start()
    rims = bottom_ref[...] * lower_ref[...] + prod_ref[...] * upper_ref[...]
    total = jnp.sum(part_ref[...] + jnp.sum(rims, axis=0, keepdims=True), axis=1, keepdims=True)
    total = jnp.broadcast_to(total, (1, LANES))
    sum_ref[...] = total
    put_sum(slots, total, outs)
    gather_blocks(slots, plane_ref, cell_refs, outs)
    copy.wait()


def repick_kernel(slots, chunks, plane_ref, sum_ref, *rest):
    cell_refs, outs = rest[:chunks], rest[chunks:]
    put_sum(slots, sum_ref[...], outs)
    gather_blocks(slots, plane_ref, cell_refs, outs)


def unpacked(slots, firsts, pos, chunks, total):
    lane = lax.broadcasted_iota(I32, pos.shape, 1).astype(F32)
    wide = min(slots, LANES)

    def one(ref, i, block, total):
        for start in range(0, slots, wide):
            base = jnp.asarray(block * slots + start, I32).astype(F32)
            chosen = (pos - base == lane).astype(F32).astype(BF16)
            total = total + jnp.dot(
                chosen[:, :wide], ref[i, start : start + wide], preferred_element_type=F32
            )
        return total

    return each(chunks, firsts, one, total)


def unpack_kernel(slots, firsts, pos_ref, *rest):
    chunks, (places_ref, total_ref) = rest[:-2], rest[-2:]
    count = pos_ref.shape[1]
    pos = jnp.transpose(jnp.broadcast_to(pos_ref[...], (LANES, count)).astype(F32))
    places_ref[...] = pos
    total_ref[...] = unpacked(slots, firsts, pos, chunks, jnp.zeros((count, LANES), F32))


def last_unpack_kernel(slots, firsts, places_ref, total_ref, *rest):
    chunks, out_ref = rest[:-1], rest[-1]
    out_ref[...] = unpacked(slots, firsts, places_ref[...], chunks, total_ref[...]).astype(BF16)


def sum_kernel(slots, after_ref, *rest):
    chunks, out_ref = rest[:-1], rest[-1]

    def one(ref, i, block, total):
        tail = ref[i, slots:].astype(F32)
        return total + tail[0:1] + tail[1:2] + tail[2:3]

    out_ref[...] = each(chunks, None, one, jnp.zeros((1, LANES), F32))


def shape_of(shape, dtype):
    return jax.ShapeDtypeStruct(shape, dtype)


def params(mib):
    return pltpu.CompilerParams(vmem_limit_bytes=mib << 20)


def in_hbm(*arrays):
    return [pltpu.with_memory_space_constraint(array, pltpu.HBM) for array in arrays]


def call(kernel, args, in_specs, out_shape, out_specs, scratch=(), aliases=None, us=1.0):
    return pl.pallas_call(
        kernel,
        out_shape=tuple(out_shape),
        in_specs=list(in_specs),
        out_specs=tuple(out_specs),
        scratch_shapes=list(scratch),
        input_output_aliases=aliases or {},
        compiler_params=params(8),
        cost_estimate=pl.CostEstimate(
            flops=0, bytes_accessed=int(us * HBM_BYTES_PER_US), transcendentals=0
        ),
    )(*args)


def shards(tdi_data, noise_diag, noise_off, src_blocks, owner_dev, layer_in, seg_in):
    groups = lax.axis_size("band") * lax.axis_size("tm")
    _, layers, segs, bins = tdi_data.shape
    count = src_blocks.shape[0]
    slots = 2 * count // groups
    halves = halves_of(slots)
    cell_count = layers * segs
    direct = groups == 8
    if direct:
        order = [7, 6, 5, 2, 3, 4, 1]
        sizes, first_out = [1] * groups, order + [0]
        first_back, second_back = order, [0]
        first_in, second_in, last_in = [0] + order[:2], order[2:4], order[4:]
        early, late = [0] + order[:5], order[5:]
    else:
        sizes, first_out = [groups], [0]
        first_back, second_back = [0], []
        first_in, second_in, last_in = [0], [], []
        early, late = [], [0]
    total = len(sizes)

    def exchanged(number, block):
        if not direct:
            return lax.all_to_all(block, AXES, split_axis=0, concat_axis=0, tiled=True)
        if number == 0:
            return block
        return lax.ppermute(block, AXES, [(i, i ^ number) for i in range(groups)])

    blocks = [shape_of((size, slots + TAIL, bins), BF16) for size in sizes]
    plane = pltpu.VMEM((cell_count, bins), F32)
    rim = shape_of((segs, bins), F32)
    line = shape_of((1, bins), F32)
    tdi = tdi_data.reshape(cell_count, bins)
    diag = noise_diag.reshape(cell_count, bins)
    off = noise_off.reshape(cell_count, bins)

    arrived = [None] * total
    resid, pos, *packed = call(
        functools.partial(pack_kernel, slots, groups, direct, first_out),
        in_hbm(
            owner_dev.reshape(1, count),
            layer_in.reshape(1, count),
            seg_in.reshape(1, count),
            src_blocks.reshape(count, bins),
            tdi,
        ),
        [HBM] * 5,
        [plane, pltpu.VMEM((1, count), I32)] + [blocks[k] for k in first_out],
        [VMEM] * (2 + len(first_out)),
        [pltpu.VMEM((1, count), I32)] * 3
        + [pltpu.VMEM((count, 2 * bins), BF16), pltpu.SemaphoreType.DMA((5,))],
        us=3.0,
    )
    for k, block in zip(first_out, packed):
        arrived[k] = exchanged(k, block)

    cells = [None] * total

    def scratch_of(step):
        size = sum(sizes[k] for k in step)
        return [
            pltpu.VMEM((size * slots, bins), F32),
            pltpu.SMEM((size * halves, LANES), I32),
            pltpu.SemaphoreType.DMA,
        ]

    def lines_of(step):
        return shape_of((sum(sizes[k] for k in step) * halves, LANES), I32)

    def split_lines(step, joined):
        start = 0
        for k in step:
            stop = start + sizes[k] * halves
            cells[k] = joined[start:stop]
            start = stop

    resid, extra, diag_in, low, high, off_last, joined = call(
        functools.partial(first_scatter_kernel, slots, segs),
        [resid] + in_hbm(diag, off) + [arrived[k] for k in first_in],
        [VMEM] + [HBM] * 2 + [VMEM] * len(first_in),
        [plane] * 3 + [rim] * 3 + [lines_of(first_in)],
        [VMEM] * 7,
        scratch_of(first_in) + [pltpu.SemaphoreType.DMA((2,))],
        {0: 0},
        us=2.5,
    )
    split_lines(first_in, joined)
    if second_in:
        resid, extra, joined = call(
            functools.partial(scatter_kernel, slots, segs),
            [resid, extra] + [arrived[k] for k in second_in],
            [VMEM] * (2 + len(second_in)),
            [plane] * 2 + [lines_of(second_in)],
            [VMEM] * 3,
            scratch_of(second_in),
            {0: 0, 1: 1},
            us=0.9,
        )
        split_lines(second_in, joined)
    bottom, product = call(
        functools.partial(rim_kernel, slots, layers),
        [joined, low, high, off_last, *arrived],
        [VMEM] * (4 + total),
        (rim, rim),
        (VMEM, VMEM),
        us=0.3,
    )
    lower_rim = passed_along(product, "band", 1)
    upper_rim = passed_along(bottom, "band", -1)
    step = last_in or [0]
    resid, extra, off_in, joined = call(
        functools.partial(last_scatter_kernel, slots, segs),
        [resid, extra] + in_hbm(off) + [arrived[k] for k in last_in],
        [VMEM] * 2 + [HBM] + [VMEM] * len(last_in),
        [plane] * 3 + [lines_of(step)],
        [VMEM] * 4,
        scratch_of(step) + [pltpu.SemaphoreType.DMA],
        {0: 0, 1: 1},
        us=2.5,
    )
    if last_in:
        split_lines(last_in, joined)
    weighed, part = call(
        functools.partial(weigh_kernel, segs, layers),
        (resid, extra, diag_in, off_in),
        [VMEM] * 4,
        (plane, line),
        (VMEM, VMEM),
        us=2.4,
    )
    returned = [None] * total
    weighed, weighted, summed, *picked = call(
        functools.partial(pick_kernel, slots, len(first_back)),
        (weighed, part, lower_rim, upper_rim, off_last, bottom, product)
        + tuple(cells[k] for k in first_back),
        [VMEM] * 7 + [SMEM] * len(first_back),
        [plane, shape_of((cell_count, bins), F32), line] + [blocks[k] for k in first_back],
        [VMEM, HBM, VMEM] + [VMEM] * len(first_back),
        [pltpu.SemaphoreType.DMA],
        {0: 0},
        us=2.5,
    )
    for k, block in zip(first_back, picked):
        returned[k] = exchanged(k, block)
    if second_back:
        picked = call(
            functools.partial(repick_kernel, slots, len(second_back)),
            (weighed, summed) + tuple(cells[k] for k in second_back),
            [VMEM] * 2 + [SMEM] * len(second_back),
            [blocks[k] for k in second_back],
            [VMEM] * len(second_back),
            us=0.5,
        )
        for k, block in zip(second_back, picked):
            returned[k] = exchanged(k, block)

    places, grads = call(
        functools.partial(unpack_kernel, slots, early),
        [pos] + [returned[k] for k in early],
        [VMEM] * (1 + len(early)),
        [pltpu.VMEM((count, LANES), F32)] * 2,
        (VMEM, VMEM),
    )
    (total_sum,) = call(
        functools.partial(sum_kernel, slots),
        [places] + returned,
        [VMEM] * (1 + total),
        (line,),
        (VMEM,),
        us=0.1,
    )
    chan = lax.axis_size("chan")
    other_sum = lax.ppermute(total_sum, "chan", [(i, i ^ 1) for i in range(chan)])
    cells_all = chan * groups * cell_count * bins
    log_like = (total_sum + other_sum)[0, :1] * (-0.5 / cells_all)
    (grads,) = call(
        functools.partial(last_unpack_kernel, slots, late),
        [places, grads] + [returned[k] for k in late],
        [VMEM] * (2 + len(late)),
        (shape_of((count, bins), BF16),),
        (VMEM,),
    )
    return (
        weighted.reshape(tdi_data.shape),
        log_like,
        grads.reshape(src_blocks.shape),
    )


def solution(mesh):
    planes = P(("grp", "chan"), "band", "tm", None)
    lists = P(("grp", "band", "tm"))
    return jax.shard_map(
        shards,
        mesh=mesh,
        in_specs=(
            planes,
            planes,
            planes,
            P(("grp", "band", "tm"), "chan", None),
            P(("grp", "band", "tm"), None),
            lists,
            lists,
        ),
        out_specs=(planes, P("grp"), P(("grp", "band", "tm"), "chan", None)),
        check_vma=False,
    )
```
